256 devices in a mesh: head: 8 (over z_lo, y), ctx: 32 (over z_hi, x, core).
Axes of the slice: x: 4, y: 4, z: 8 (z_hi: 4, z_lo: 2; z = z_hi * 2 + z_lo), core: 2. Of those that a mesh axis runs over, the one named last changes fastest.
Arguments:
- queries: bfloat16 [512, 24576], P(None, 'head'), may hold values from -100 to 100
- attn_keys: bfloat16 [8192, 24576], P('ctx', 'head'), may hold values from -6 to 6
- index_queries: bfloat16 [512, 8192], P(None, 'head'), may hold values from -16 to 16
- index_keys: bfloat16 [8192, 128], P('ctx'), may hold values from -6 to 6
- head_weights: float32 [512, 64], P(None, 'head'), may hold values from 0.1 to 1
- query_pos: int32 [512], replicated, may hold values from 16 to 65535
- key_offset: int32 [8192], P('ctx'), may hold values from 0 to 7
Outputs:
- index_query_grad: float32 [512, 8192], P('ctx', 'head')
- index_key_grad: float32 [8192, 128], P('ctx')
The draws below stay inside these ranges and needn't reach their ends.
All inputs are finite; a program needn't handle non-finite values.
Results may differ from the reference program's by a relative error of at most 0.0027.
Values sent between devices are 32-bit elements; how exact they have to be, the bound alone decides.
No kernel may reach another device: no remote copies, remote signals or barrier semaphores. Data moves between devices by JAX's collectives and lax.ppermute only.
A program may use at most 64 MiB of HBM per device.

```python
import math
import jax
import jax.numpy as jnp
from jax import lax

HEADS = 128
HEAD_DIM = 192
IHEADS = 64
IDIM = 128
QUERIES = 512
STRIDE = 8
KEYS = 8192


def attn_keys_base(key):
    sub_key = jax.random.fold_in(key, 101)
    base = jnp.clip(jax.random.normal(sub_key, (KEYS, HEADS * HEAD_DIM), jnp.float32), -6.0, 6.0)
    return base


def index_keys_base(key):
    sub_key = jax.random.fold_in(key, 103)
    base = jnp.clip(jax.random.normal(sub_key, (KEYS, IDIM), jnp.float32), -6.0, 6.0)
    return base


def draw_attn_keys(key, part):
    return attn_keys_base(key).astype(jnp.bfloat16)


def draw_index_keys(key, part):
    return index_keys_base(key).astype(jnp.bfloat16)


def draw_queries(key, part):
    sub_key = jax.random.fold_in(key, 102)
    base = jnp.clip(jax.random.normal(sub_key, (QUERIES, HEADS * HEAD_DIM), jnp.float32), -6.0, 6.0)
    return base.astype(jnp.bfloat16)


def draw_index_queries(key, part):
    sub_key = jax.random.fold_in(key, 104)
    base = jnp.clip(jax.random.normal(sub_key, (QUERIES, IHEADS * IDIM), jnp.float32), -6.0, 6.0)
    return base.astype(jnp.bfloat16)


def place_ends(array, key, smallest, high):
    extent = array.shape
    spot = [jax.random.randint(jax.random.fold_in(key, axis), (), 0, extent[axis]) for axis in range(len(extent))]
    array = array.at[tuple(spot)].set(smallest)
    longest = extent.index(max(extent))
    spot[longest] = (spot[longest] + 1) % extent[longest]
    return array.at[tuple(spot)].set(high)


def block_scale(rng, extent, split, smallest, high):
    level = 1.0
    for axis_at, blocks in split:
        draws = jax.random.uniform(jax.random.fold_in(jax.random.fold_in(rng, 6), axis_at), (blocks,), jnp.float32, smallest / len(split), high / len(split))
        level = level * jnp.repeat(jnp.exp(draws), extent[axis_at] // blocks).reshape((-1,) + (1,) * (len(extent) - 1 - axis_at))
    return level


def setup_inputs(seed: int = 0) -> dict:
    streams_of = jax.random.split(jax.random.key(seed), 8)
    return {
        "queries": draw_queries(jax.random.fold_in(streams_of[7], 71), 0),
        "attn_keys": draw_attn_keys(jax.random.fold_in(streams_of[7], 71), 0),
        "index_queries": draw_index_queries(jax.random.fold_in(streams_of[7], 71), 0),
        "index_keys": draw_index_keys(jax.random.fold_in(streams_of[7], 71), 0),
        "head_weights": jnp.clip(jnp.exp(math.log(1.0) - 2.3025851 * jax.random.uniform(streams_of[4], (QUERIES, IHEADS), jnp.float32) ** block_scale(streams_of[4], (QUERIES, IHEADS), ((1, 8),), -0.2, 0.2)), 0.1, 1.0),
        "query_pos": place_ends(jax.random.randint(streams_of[5], (QUERIES,), 2 * STRIDE, STRIDE * KEYS), jax.random.fold_in(streams_of[5], 1), 2 * STRIDE, (STRIDE * KEYS) - 1).astype(jnp.int32),
        "key_offset": place_ends(jax.random.randint(streams_of[6], (KEYS,), 0, STRIDE), jax.random.fold_in(streams_of[6], 1), 0, STRIDE - 1).astype(jnp.int32),
    }


NEG_FILL = -1e+30

def reference(queries, attn_keys, index_queries, index_keys, head_weights, query_pos, key_offset):
    key_pos = STRIDE * jnp.arange(KEYS, dtype=jnp.int32) + key_offset
    visible = key_pos[None, :] <= query_pos[:, None]
    attn_scale = 1.0 / math.sqrt(HEAD_DIM)
    inv_scale = 1.0 / math.sqrt(IDIM)

    def attn_head(total, head_index):
        start = (head_index * HEAD_DIM).astype(jnp.int32)
        query_head = lax.dynamic_slice_in_dim(queries, start, HEAD_DIM, 1)
        key_head = lax.dynamic_slice_in_dim(attn_keys, start, HEAD_DIM, 1)
        scores = jnp.dot(query_head, key_head.T, preferred_element_type=jnp.float32) * attn_scale
        masked = jnp.where(visible, scores, NEG_FILL)
        top_value = lax.optimization_barrier(jnp.max(masked, axis=1, keepdims=True))
        exp_terms = jnp.where(visible, jnp.exp(masked - top_value), 0.0)
        return (total + exp_terms / lax.optimization_barrier(jnp.sum(exp_terms, axis=1, keepdims=True)), None)
    total, _ = lax.scan(attn_head, jnp.zeros((QUERIES, KEYS), jnp.float32), jnp.arange(HEADS, dtype=jnp.int32))
    target = total / HEADS

    def index_slices(head_index):
        start = (head_index * IDIM).astype(jnp.int32)
        query_head = lax.dynamic_slice_in_dim(index_queries, start, IDIM, 1)
        activation = jnp.dot(query_head, index_keys.T, preferred_element_type=jnp.float32) * inv_scale
        weight_col = lax.dynamic_slice_in_dim(head_weights, head_index.astype(jnp.int32), 1, 1)
        return (query_head, activation, weight_col)

    def index_head(logits, head_index):
        query_head, activation, weight_col = index_slices(head_index)
        return (logits + weight_col * jnp.maximum(activation, 0.0), None)
    logits, _ = lax.scan(index_head, jnp.zeros((QUERIES, KEYS), jnp.float32), jnp.arange(IHEADS, dtype=jnp.int32))
    masked = jnp.where(visible, logits, NEG_FILL)
    top_value = lax.optimization_barrier(jnp.max(masked, axis=1, keepdims=True))
    exp_terms = jnp.where(visible, jnp.exp(masked - top_value), 0.0)
    prob_step = exp_terms / lax.optimization_barrier(jnp.sum(exp_terms, axis=1, keepdims=True)) - target

    def grad_head(key_grad, head_index):
        query_head, activation, weight_col = index_slices(head_index)
        grad_terms = jnp.where(activation > 0.0, prob_step * weight_col * inv_scale, 0.0).astype(jnp.bfloat16)
        query_grad = jnp.dot(grad_terms, index_keys, preferred_element_type=jnp.float32)
        key_grad = key_grad + jnp.dot(grad_terms.T, query_head, preferred_element_type=jnp.float32)
        return (key_grad, query_grad)
    key_grad, query_stack = lax.scan(grad_head, jnp.zeros((KEYS, IDIM), jnp.float32), jnp.arange(IHEADS, dtype=jnp.int32))
    query_grad = jnp.transpose(query_stack, (1, 0, 2)).reshape(QUERIES, IHEADS * IDIM)
    return (query_grad, key_grad)
```

```python
import math

import jax
import jax.numpy as jnp
from jax import lax
from jax.experimental import pallas as pl
from jax.experimental.pallas import tpu as pltpu
from jax.sharding import Mesh
from jax.sharding import PartitionSpec as P

HEADS = 128
HEAD_DIM = 192
IDIM = 128
STRIDE = 8
LANES = 128
LOG2E = math.log2(math.e)
NEG_FILL = -1e30
SCORE_SCALE = LOG2E / math.sqrt(HEAD_DIM)
INV_SCALE = 1.0 / math.sqrt(IDIM)

AXES = ("z_lo", "y", "z_hi", "x", "core")
HEAD = ("z_lo", "y")
CTX = ("z_hi", "x", "core")
CHIP = ("z_hi", "x")
F32, BF16 = jnp.float32, jnp.bfloat16
VMEM_SPEC = pl.BlockSpec(memory_space=pltpu.VMEM)
SMEM_SPEC = pl.BlockSpec(memory_space=pltpu.SMEM)
PARAMS = pltpu.CompilerParams(vmem_limit_bytes=40 * 2**20)


def shift(value, axis, size, step):
    return lax.ppermute(value, axis, [(i, (i + step) % size) for i in range(size)])


def merge(parts):
    top = jnp.max(parts, axis=0)
    return top + jnp.log2(jnp.sum(jnp.exp2(parts - top[None]), axis=0))


def dot_t(a, b):
    return lax.dot_general(a, b, (((1,), (1,)), ((), ())), preferred_element_type=F32)


def head_scores(q_ref, k_ref, which):
    lane = lax.broadcasted_iota(jnp.int32, (1, LANES), 1)
    low = (lane < HEAD_DIM - LANES).astype(F32)
    if which == 0:
        k = jnp.concatenate([k_ref[:, :LANES], k_ref[:, LANES : 2 * LANES] * low.astype(BF16)], axis=1)
        q = q_ref[:, : 2 * LANES]
    else:
        k = jnp.concatenate(
            [k_ref[:, LANES : 2 * LANES] * (1.0 - low).astype(BF16), k_ref[:, 2 * LANES :]], axis=1
        )
        q = q_ref[:, LANES:]
    return dot_t(k, q) * SCORE_SCALE


def fill_bias(bias, kp_ref, qp_ref):
    bias[...] = jnp.where(kp_ref[...] <= qp_ref[...], 0.0, NEG_FILL)


def lse_kernel(sc_ref, q_ref, k_ref, kp_ref, qp_ref, mine_ref, other_ref, bias):
    i = pl.program_id(0)

    @pl.when(i == 0)
    def _():
        fill_bias(bias, kp_ref, qp_ref)

    half_steps = mine_ref.shape[0] // 2
    for which in range(2):
        s = head_scores(q_ref, k_ref, which) + bias[...]
        top = jnp.max(s, axis=0, keepdims=True)
        value = top + jnp.log2(jnp.sum(jnp.exp2(s - top), axis=0, keepdims=True))
        row = pl.ds(2 * lax.rem(i, half_steps) + which, 1)

        @pl.when(i // half_steps == sc_ref[0])
        def _():
            mine_ref[row, :] = value

        @pl.when(i // half_steps != sc_ref[0])
        def _():
            other_ref[row, :] = value


def pair_specs(rows, keys):
    width = 2 * HEAD_DIM
    return [
        SMEM_SPEC,
        pl.BlockSpec((rows, width), lambda i: (0, i)),
        pl.BlockSpec((keys, width), lambda i: (0, i)),
        pl.BlockSpec((keys, 1), lambda i: (0, 0)),
        pl.BlockSpec((1, rows), lambda i: (0, 0)),
    ]


def scores_lse(sc, queries, attn_keys, kp, qp):
    rows, keys = queries.shape[0], attn_keys.shape[0]
    heads = queries.shape[1] // HEAD_DIM
    out = jax.ShapeDtypeStruct((heads // 2, rows), F32)
    spec = pl.BlockSpec((heads // 2, rows), lambda i: (0, 0))
    return pl.pallas_call(
        lse_kernel,
        grid=(heads // 2,),
        in_specs=pair_specs(rows, keys),
        out_specs=[spec, spec],
        out_shape=[out, out],
        scratch_shapes=[pltpu.VMEM((keys, rows), F32)],
        compiler_params=PARAMS,
        name="scores_lse",
    )(sc, queries, attn_keys, kp, qp)


def split_rows(tr, out_ref, value):
    turned = value.T
    n, blk, keys = out_ref.shape
    for half in range(keys // LANES):
        span = slice(half * LANES, (half + 1) * LANES)
        tr[half * n * blk : (half + 1) * n * blk, :] = turned[:, span]
        for h in range(n):
            out_ref[h, :, span] = tr[pl.ds(half * n * blk + h, blk, stride=n), :]


def probs_kernel(sc_ref, q_ref, k_ref, kp_ref, qp_ref, mine_ref, other_ref, out_ref, bias, acc, tr):
    i = pl.program_id(0)

    @pl.when(i == 0)
    def _():
        fill_bias(bias, kp_ref, qp_ref)
        acc[...] = jnp.zeros_like(acc)

    half_steps = mine_ref.shape[0] // 2
    own = i // half_steps == sc_ref[0]
    total = acc[...]
    for which in range(2):
        row = pl.ds(2 * lax.rem(i, half_steps) + which, 1)
        lse = jnp.where(own, mine_ref[row, :], other_ref[row, :])
        total += jnp.exp2(head_scores(q_ref, k_ref, which) + bias[...] - lse)
    acc[...] = total

    @pl.when(i == pl.num_programs(0) - 1)
    def _():
        split_rows(tr, out_ref, acc[...])


def probs_sum(sc, queries, attn_keys, kp, qp, mine, other, n_head):
    rows, keys = queries.shape[0], attn_keys.shape[0]
    heads = queries.shape[1] // HEAD_DIM
    spec = pl.BlockSpec(mine.shape, lambda i: (0, 0))
    shape = (n_head, rows // n_head, keys)
    return pl.pallas_call(
        probs_kernel,
        grid=(heads // 2,),
        in_specs=pair_specs(rows, keys) + [spec, spec],
        out_specs=pl.BlockSpec(shape, lambda i: (0, 0, 0)),
        out_shape=jax.ShapeDtypeStruct(shape, F32),
        scratch_shapes=[
            pltpu.VMEM((keys, rows), F32),
            pltpu.VMEM((keys, rows), F32),
            pltpu.VMEM((rows * keys // LANES, LANES), F32),
        ],
        compiler_params=PARAMS,
        name="probs_sum",
    )(sc, queries, attn_keys, kp, qp, mine, other)


def logits_kernel(iq_ref, ik_ref, w_ref, out_ref, tr):
    total = None
    for j in range(w_ref.shape[0]):
        act = dot_t(ik_ref[...], iq_ref[:, j * IDIM : (j + 1) * IDIM])
        term = jnp.maximum(act, 0.0) * w_ref[j : j + 1, :]
        total = term if total is None else total + term
    split_rows(tr, out_ref, total)


def part_logits(iq, ik, w, n_head):
    rows, keys = iq.shape[0], ik.shape[0]
    return pl.pallas_call(
        logits_kernel,
        in_specs=[VMEM_SPEC] * 3,
        out_specs=VMEM_SPEC,
        out_shape=jax.ShapeDtypeStruct((n_head, rows // n_head, keys), F32),
        scratch_shapes=[pltpu.VMEM((rows * keys // LANES, LANES), F32)],
        compiler_params=PARAMS,
        name="part_logits",
    )(iq, ik, w)


def merge_kernel(parts_ref, out_ref):
    out_ref[...] = merge(parts_ref[...])


def merge_parts(parts):
    return pl.pallas_call(
        merge_kernel,
        in_specs=[VMEM_SPEC],
        out_specs=VMEM_SPEC,
        out_shape=jax.ShapeDtypeStruct(parts.shape[1:], F32),
        name="merge_parts",
    )(parts)


def step_kernel(target_ref, logits_ref, lse_ref, wide_ref, chips_ref, tmp):
    target = jnp.sum(target_ref[...], axis=0) * (1.0 / HEADS)
    blk = target.shape[0]
    lse = merge(lse_ref[...]).T[:blk, :1]
    step = jnp.exp2(logits_ref[...] - lse) - target
    for h in range(wide_ref.shape[0]):
        wide_ref[h] = step
    n_chip, per = chips_ref.shape[0], chips_ref.shape[1] // 2
    for half in range(2):
        tmp[half * blk : (half + 1) * blk, :] = step[:, half * LANES : (half + 1) * LANES]
        for r in range(per):
            chips_ref[:, half * per + r, :] = tmp[pl.ds(half * blk + r, n_chip, stride=per), :]


def prob_step(target_parts, logits, lse_parts, n_chip):
    n_head, blk, keys = target_parts.shape
    return pl.pallas_call(
        step_kernel,
        in_specs=[VMEM_SPEC] * 3,
        out_specs=[VMEM_SPEC] * 2,
        out_shape=[
            jax.ShapeDtypeStruct((n_head, blk, keys), F32),
            jax.ShapeDtypeStruct((n_chip, 2 * blk // n_chip, LANES), F32),
        ],
        scratch_shapes=[pltpu.VMEM((blk * keys // LANES, LANES), F32)],
        name="prob_step",
    )(target_parts, logits, lse_parts)


def key_kernel(step_ref, iq_ref, ik_ref, w_ref, out_ref, tr):
    n, blk, keys = step_ref.shape
    turned = []
    for half in range(keys // LANES):
        base = half * n * blk
        for h in range(n):
            tr[pl.ds(base + h, blk, stride=n), :] = step_ref[h, :, half * LANES : (half + 1) * LANES]
        turned.append(tr[base : base + n * blk, :].T)
    step = jnp.concatenate(turned, axis=0)
    total = None
    for j in range(w_ref.shape[0]):
        iq = iq_ref[:, j * IDIM : (j + 1) * IDIM]
        act = dot_t(ik_ref[...], iq)
        terms = jnp.where(act > 0.0, step * (w_ref[j : j + 1, :] * INV_SCALE), 0.0).astype(BF16)
        part = jnp.dot(terms, iq, preferred_element_type=F32)
        total = part if total is None else total + part
    out_ref[...] = total


def key_part_grad(step, iq, ik, w):
    rows, keys = iq.shape[0], ik.shape[0]
    return pl.pallas_call(
        key_kernel,
        in_specs=[VMEM_SPEC] * 4,
        out_specs=VMEM_SPEC,
        out_shape=jax.ShapeDtypeStruct((keys, IDIM), F32),
        scratch_shapes=[pltpu.VMEM((rows * keys // LANES, LANES), F32)],
        compiler_params=PARAMS,
        name="key_part_grad",
    )(step, iq, ik, w)


def query_kernel(sc_ref, step_ref, both_ref, ik0_ref, ik1_ref, ik2_ref, ik3_ref, keep_ref, give_ref, tmp):
    n_head, pj = both_ref.shape[0], both_ref.shape[2]
    per = step_ref.shape[1] // 2
    jl = pj // per
    iq = both_ref[:, 0].reshape(n_head * pj, IDIM).astype(BF16)
    w = both_ref[:, 1].reshape(n_head * pj, LANES)
    total = None
    for dx, ik_ref in enumerate((ik0_ref, ik1_ref, ik2_ref, ik3_ref)):
        for dz in range(4):
            source = lax.rem(sc_ref[1] + 4 - dz, 4) * 4 + lax.rem(sc_ref[2] + 4 - dx, 4)
            ik = ik_ref[dz].astype(BF16)
            act = dot_t(iq, ik)
            tile = step_ref[source]
            halves = []
            for half in range(2):
                rows = [
                    jnp.broadcast_to(tile[half * per + r : half * per + r + 1, :], (jl, LANES))
                    for r in range(per)
                ]
                step = jnp.concatenate(rows * n_head, axis=0)
                halves.append(step * w)
            step = jnp.concatenate(halves, axis=1)
            terms = jnp.where(act > 0.0, step, 0.0).astype(BF16)
            part = jnp.dot(terms, ik, preferred_element_type=F32)
            total = part if total is None else total + part
    tmp[...] = total.reshape(tmp.shape)
    keep_ref[...] = tmp[:, sc_ref[0]]
    give_ref[...] = tmp[:, 1 - sc_ref[0]]


def query_part_grad(sc, step, both, blocks):
    n_head, _, pj, _ = both.shape
    out = jax.ShapeDtypeStruct((n_head, pj // 2, IDIM), F32)
    return pl.pallas_call(
        query_kernel,
        in_specs=[SMEM_SPEC] + [VMEM_SPEC] * 6,
        out_specs=[VMEM_SPEC] * 2,
        out_shape=[out, out],
        scratch_shapes=[pltpu.VMEM((n_head, 2, pj // 2, IDIM), F32)],
        compiler_params=PARAMS,
        name="query_part_grad",
    )(sc, step, both, *blocks)


def place_kernel(parts_ref, out_ref, tmp):
    n, rj, _ = parts_ref.shape
    jl = out_ref.shape[1] // IDIM
    tmp[...] = parts_ref[...].reshape(tmp.shape)
    for r in range(rj // jl):
        for j in range(jl):
            out_ref[r * n : (r + 1) * n, j * IDIM : (j + 1) * IDIM] = tmp[
                pl.ds(r * jl + j, n, stride=rj), :
            ]


def place_rows(parts, jl):
    n, rj, _ = parts.shape
    return pl.pallas_call(
        place_kernel,
        in_specs=[VMEM_SPEC],
        out_specs=VMEM_SPEC,
        out_shape=jax.ShapeDtypeStruct((n * rj // jl, jl * IDIM), F32),
        scratch_shapes=[pltpu.VMEM((n * rj, IDIM), F32)],
        name="place_rows",
    )(parts)


def shards(queries, attn_keys, index_queries, index_keys, head_weights, query_pos, key_offset):
    rows, keys = queries.shape[0], attn_keys.shape[0]
    jl = index_queries.shape[1] // IDIM
    n_head, n_chip = lax.axis_size(HEAD), lax.axis_size(CHIP)
    blk = rows // n_head
    per = blk // n_chip
    core, zi, xi = (lax.axis_index(a) for a in ("core", "z_hi", "x"))
    hd, chip = lax.axis_index(HEAD), lax.axis_index(CHIP)
    sc = jnp.stack([core, zi, xi]).astype(jnp.int32)

    key_pos = STRIDE * (lax.axis_index(CTX) * keys + jnp.arange(keys, dtype=jnp.int32)) + key_offset
    kp, qp = key_pos[:, None], query_pos[None, :]
    qp_a = lax.dynamic_index_in_dim(query_pos.reshape(blk, n_head), hd, 1, False)
    bias_a = jnp.where(key_pos[None, :] <= qp_a[:, None], 0.0, NEG_FILL)
    w_o = head_weights.T

    mine, other = scores_lse(sc, queries, attn_keys, kp, qp)
    mine = merge(jnp.stack([mine, shift(other, "core", 2, 1)]))
    mine = merge_parts(
        lax.all_to_all(jnp.broadcast_to(mine[None], (n_chip, *mine.shape)), CHIP, 0, 0)
    )
    other = shift(mine, "core", 2, 1)
    target = probs_sum(sc, queries, attn_keys, kp, qp, mine, other, n_head)
    target = lax.all_to_all(target, HEAD, 0, 0)

    logits = part_logits(index_queries, index_keys, w_o, n_head)
    logits = jnp.sum(lax.all_to_all(logits, HEAD, 0, 0), axis=0) * (LOG2E * INV_SCALE) + bias_a
    top = jnp.max(logits, axis=1)
    lse = top + jnp.log2(jnp.sum(jnp.exp2(logits - top[:, None]), axis=1))
    lse = jnp.broadcast_to(jnp.pad(lse, (0, LANES - blk))[None], (8, LANES))
    lse = merge(jnp.stack([lse, shift(lse, "core", 2, 1)]))
    lse = lax.all_to_all(jnp.broadcast_to(lse[None], (n_chip, 8, LANES)), CHIP, 0, 0)

    step_wide, step_chips = prob_step(target, logits, lse, n_chip)

    step_o = lax.all_to_all(step_wide, HEAD, 0, 0)
    key_part = key_part_grad(step_o, index_queries, index_keys, w_o)
    key_part = key_part + shift(key_part, "z_lo", 2, 1)
    key_grad = key_part
    for k in range(1, 4):
        key_grad = key_grad + shift(key_part, "y", 4, k)

    iq_b = lax.dynamic_index_in_dim(
        index_queries.reshape(n_chip, per, n_head, jl * IDIM), chip, 0, False
    ).transpose(1, 0, 2).astype(F32).reshape(n_head, per * jl, IDIM)
    w_b = lax.dynamic_index_in_dim(
        head_weights.reshape(n_chip, per, n_head, jl), chip, 0, False
    ).transpose(1, 0, 2) * INV_SCALE
    w_b = jnp.broadcast_to(w_b.reshape(n_head, per * jl, 1), iq_b.shape)
    both = lax.all_to_all(jnp.stack([iq_b, w_b], 1), HEAD, 0, 0)
    ik = index_keys.astype(F32)
    zs = jnp.stack([ik] + [shift(ik, "z_hi", 4, k) for k in range(1, 4)])
    blocks = [zs] + [shift(zs, "x", 4, k) for k in range(1, 4)]

    step_b = lax.all_to_all(step_chips, CHIP, 0, 0)
    keep, give = query_part_grad(sc, step_b, both, blocks)
    qg = keep + shift(give, "core", 2, 1)
    qg = lax.all_to_all(qg, HEAD, 0, 0)
    return (place_rows(qg, jl), key_grad)


def solution(mesh):
    mesh = Mesh(mesh.devices.reshape(2, 4, 4, 4, 2), AXES)
    in_specs = (
        P(None, HEAD),
        P(CTX, HEAD),
        P(None, HEAD),
        P(CTX, None),
        P(None, HEAD),
        P(),
        P(CTX),
    )
    out_specs = (P(CTX, HEAD), P(CTX, None))
    return jax.shard_map(shards, mesh=mesh, in_specs=in_specs, out_specs=out_specs, check_vma=False)
```

```python
import math

import jax
import jax.numpy as jnp
from jax import lax
from jax.experimental import pallas as pl
from jax.experimental.pallas import tpu as pltpu
from jax.sharding import Mesh
from jax.sharding import PartitionSpec as P

HEADS = 128
HEAD_DIM = 192
IDIM = 128
STRIDE = 8
LANES = 128
NEG_FILL = -1e30
SCORE_SCALE = 1.0 / math.sqrt(HEAD_DIM)
INV_SCALE = 1.0 / math.sqrt(IDIM)

AXES = ("z_lo", "y", "z_hi", "x", "core")
HEAD = ("z_lo", "y")
CTX = ("z_hi", "x", "core")
CHIP = ("z_hi", "x")
F32, BF16 = jnp.float32, jnp.bfloat16
VMEM_SPEC = pl.BlockSpec(memory_space=pltpu.VMEM)
SMEM_SPEC = pl.BlockSpec(memory_space=pltpu.SMEM)
ANY_SPEC = pl.BlockSpec(memory_space=pl.ANY)
PARAMS = pltpu.CompilerParams(vmem_limit_bytes=16 * 2**20)


def shift(value, axis, size, step):
    return lax.ppermute(value, axis, [(i, (i + step) % size) for i in range(size)])


def merge(parts):
    top = jnp.max(parts, axis=0)
    return top + jnp.log(jnp.sum(jnp.exp(parts - top[None]), axis=0))


def dot_t(a, b):
    return lax.dot_general(a, b, (((1,), (1,)), ((), ())), preferred_element_type=F32)


def head_scores(q_ref, k_ref, head):
    lane = lax.broadcasted_iota(jnp.int32, (1, LANES), 1)
    low = (lane < HEAD_DIM - LANES).astype(F32)
    at = head // 2 * 2 * HEAD_DIM + head % 2 * LANES
    q = q_ref[:, at : at + 2 * LANES]
    left, right = k_ref[:, at : at + LANES], k_ref[:, at + LANES : at + 2 * LANES]
    if head % 2 == 0:
        right = right * low.astype(BF16)
    else:
        left = left * (1.0 - low).astype(BF16)
    return dot_t(jnp.concatenate([left, right], axis=1), q) * SCORE_SCALE


def fill_bias(bias, kp_ref, qp_ref):
    bias[...] = jnp.where(kp_ref[...] <= qp_ref[...], 0.0, NEG_FILL)


def fetch(q_hbm, k_hbm, q_ref, k_ref, sems):
    width = 2 * HEAD_DIM
    copies = []
    for i in range(q_hbm.shape[1] // width):
        span = pl.ds(i * width, width)
        pair = [
            pltpu.make_async_copy(q_hbm.at[:, span], q_ref.at[:, span], sems.at[0, i]),
            pltpu.make_async_copy(k_hbm.at[:, span], k_ref.at[:, span], sems.at[1, i]),
        ]
        for copy in pair:
            copy.start()
        copies.append(pair)

    def wait(i):
        for copy in copies[i]:
            copy.wait()

    return wait


def lse_kernel(q_hbm, k_hbm, kp_ref, qp_ref, out_ref, q_ref, k_ref, sems, bias):
    wait = fetch(q_hbm, k_hbm, q_ref, k_ref, sems)
    fill_bias(bias, kp_ref, qp_ref)
    for head in range(out_ref.shape[0]):
        if head % 2 == 0:
            wait(head // 2)
        s = head_scores(q_ref, k_ref, head) + bias[...]
        top = jnp.max(s, axis=0, keepdims=True)
        out_ref[head : head + 1, :] = top + jnp.log(jnp.sum(jnp.exp(s - top), axis=0, keepdims=True))


def fetch_scratch(queries, attn_keys):
    pairs = queries.shape[1] // (2 * HEAD_DIM)
    return [
        pltpu.VMEM(queries.shape, BF16),
        pltpu.VMEM(attn_keys.shape, BF16),
        pltpu.SemaphoreType.DMA((2, pairs)),
        pltpu.VMEM((attn_keys.shape[0], queries.shape[0]), F32),
    ]


def scores_lse(queries, attn_keys, kp, qp):
    rows = queries.shape[0]
    heads = queries.shape[1] // HEAD_DIM
    return pl.pallas_call(
        lse_kernel,
        in_specs=[ANY_SPEC] * 2 + [VMEM_SPEC] * 2,
        out_specs=VMEM_SPEC,
        out_shape=jax.ShapeDtypeStruct((heads, rows), F32),
        scratch_shapes=fetch_scratch(queries, attn_keys),
        compiler_params=PARAMS,
        name="scores_lse",
    )(queries, attn_keys, kp, qp)


def index_logits(parts_ref, kp_ref, qp_ref):
    logits = jnp.sum(parts_ref[...], axis=0) * INV_SCALE
    return logits + jnp.where(kp_ref[...] <= qp_ref[...], 0.0, NEG_FILL)


def join_kernel(sc_ref, lse_ref, parts_ref, kp_ref, qp_ref, keep_ref, give_ref):
    half, rows = lse_ref.shape[0] // 2, lse_ref.shape[1]
    logits = index_logits(parts_ref, kp_ref, qp_ref)
    blk, _ = logits.shape
    top = jnp.max(logits, axis=1, keepdims=True)
    value = top + jnp.log(jnp.sum(jnp.exp(logits - top), axis=1, keepdims=True))
    value = jnp.broadcast_to(value, (blk, LANES))
    value = jnp.concatenate([value, jnp.zeros((LANES - blk, LANES), F32)], axis=0).T
    for out_ref, core in ((keep_ref, sc_ref[0]), (give_ref, 1 - sc_ref[0])):
        out_ref[:, :rows] = lse_ref[pl.ds(pl.multiple_of(core * half, half), half), :]
        out_ref[:, rows:] = value[:half]


def join_lse(sc, lse, parts, kp_row, qp_a):
    heads, rows = lse.shape
    out = jax.ShapeDtypeStruct((heads // 2, rows + LANES), F32)
    return pl.pallas_call(
        join_kernel,
        in_specs=[SMEM_SPEC] + [VMEM_SPEC] * 4,
        out_specs=[VMEM_SPEC] * 2,
        out_shape=[out, out],
        compiler_params=PARAMS,
        name="join_lse",
    )(sc, lse, parts, kp_row, qp_a)


def pair_kernel(mine_ref, got_ref, out_ref):
    both = merge(jnp.stack([mine_ref[...], got_ref[...]]))
    for c in range(out_ref.shape[0]):
        out_ref[c] = both


def pair_merge(mine, got, n_chip):
    return pl.pallas_call(
        pair_kernel,
        in_specs=[VMEM_SPEC] * 2,
        out_specs=VMEM_SPEC,
        out_shape=jax.ShapeDtypeStruct((n_chip, *mine.shape), F32),
        compiler_params=PARAMS,
        name="pair_merge",
    )(mine, got)


def merge_kernel(parts_ref, out_ref):
    out_ref[...] = merge(parts_ref[...])


def merge_parts(parts):
    return pl.pallas_call(
        merge_kernel,
        in_specs=[VMEM_SPEC],
        out_specs=VMEM_SPEC,
        out_shape=jax.ShapeDtypeStruct(parts.shape[1:], F32),
        compiler_params=PARAMS,
        name="merge_parts",
    )(parts)


def split_rows(tr, out_ref, value):
    turned = value.T
    n, blk, keys = out_ref.shape
    for half in range(keys // LANES):
        span = slice(half * LANES, (half + 1) * LANES)
        tr[half * n * blk : (half + 1) * n * blk, :] = turned[:, span]
        for h in range(n):
            out_ref[h, :, span] = tr[pl.ds(half * n * blk + h, blk, stride=n), :]


def probs_kernel(sc_ref, q_hbm, k_hbm, kp_ref, qp_ref, mine_ref, other_ref, out_ref, q_ref, k_ref, sems, bias, lse, tr):
    wait = fetch(q_hbm, k_hbm, q_ref, k_ref, sems)
    fill_bias(bias, kp_ref, qp_ref)
    half, rows = mine_ref.shape[0], lse.shape[1]
    for ref, core in ((mine_ref, sc_ref[0]), (other_ref, 1 - sc_ref[0])):
        lse[pl.ds(pl.multiple_of(core * half, half), half), :] = ref[:, :rows]
    total = None
    for head in range(0, lse.shape[0], 2):
        wait(head // 2)
        pair = [
            jnp.exp(head_scores(q_ref, k_ref, h) + bias[...] - lse[h : h + 1, :]) for h in (head, head + 1)
        ]
        total = pair[0] + pair[1] if total is None else total + (pair[0] + pair[1])
    split_rows(tr, out_ref, total)


def probs_sum(sc, queries, attn_keys, kp, qp, mine, other, n_head):
    rows, keys = queries.shape[0], attn_keys.shape[0]
    heads = queries.shape[1] // HEAD_DIM
    return pl.pallas_call(
        probs_kernel,
        in_specs=[SMEM_SPEC] + [ANY_SPEC] * 2 + [VMEM_SPEC] * 4,
        out_specs=VMEM_SPEC,
        out_shape=jax.ShapeDtypeStruct((n_head, rows // n_head, keys), F32),
        scratch_shapes=fetch_scratch(queries, attn_keys)
        + [pltpu.VMEM((heads, rows), F32), pltpu.VMEM((rows * keys // LANES, LANES), F32)],
        compiler_params=PARAMS,
        name="probs_sum",
    )(sc, queries, attn_keys, kp, qp, mine, other)


def logits_kernel(iq_ref, ik_ref, wt_ref, out_ref, wide_ref, tr):
    total = None
    for j in range(wt_ref.shape[0]):
        act = dot_t(ik_ref[...], iq_ref[:, j * IDIM : (j + 1) * IDIM])
        term = jnp.maximum(act, 0.0) * wt_ref[j : j + 1, :]
        total = term if total is None else total + term
    split_rows(tr, out_ref, total)
    wide_ref[...] = ik_ref[...].astype(F32)


def part_logits(iq, ik, wt, n_head):
    rows, keys = iq.shape[0], ik.shape[0]
    return pl.pallas_call(
        logits_kernel,
        in_specs=[VMEM_SPEC] * 3,
        out_specs=[VMEM_SPEC] * 2,
        out_shape=[
            jax.ShapeDtypeStruct((n_head, rows // n_head, keys), F32),
            jax.ShapeDtypeStruct(ik.shape, F32),
        ],
        scratch_shapes=[pltpu.VMEM((rows * keys // LANES, LANES), F32)],
        compiler_params=PARAMS,
        name="part_logits",
    )(iq, ik, wt)


def step_kernel(sc_ref, target_ref, index_ref, lse_ref, kp_ref, qp_ref, keep_ref, give_ref, tmp):
    target = jnp.sum(target_ref[...], axis=0) * (1.0 / HEADS)
    blk, keys = target.shape
    rows = lse_ref.shape[1] - LANES
    lse = lse_ref[:8, rows:].T[:blk, :1]
    step = jnp.exp(index_logits(index_ref, kp_ref, qp_ref) - lse) - target
    for half in range(keys // LANES):
        span = slice(half * LANES, (half + 1) * LANES)
        tmp[half * blk : (half + 1) * blk, :] = step[:, span]
        for out_ref, core in ((keep_ref, sc_ref[0]), (give_ref, 1 - sc_ref[0])):
            for x in range(4):
                for r in range(2):
                    out_ref[half, pl.ds(8 * x + r, 4, stride=2), :] = tmp[
                        pl.ds(half * blk + 4 * x + 2 * core + r, 4, stride=16), :
                    ]


def prob_step(sc, target_parts, index_parts, lse, kp_row, qp_a):
    _, blk, keys = target_parts.shape
    out = jax.ShapeDtypeStruct((keys // LANES, blk // 2, LANES), F32)
    return pl.pallas_call(
        step_kernel,
        in_specs=[SMEM_SPEC] + [VMEM_SPEC] * 5,
        out_specs=[VMEM_SPEC] * 2,
        out_shape=[out, out],
        scratch_shapes=[pltpu.VMEM((blk * keys // LANES, LANES), F32)],
        compiler_params=PARAMS,
        name="prob_step",
    )(sc, target_parts, index_parts, lse, kp_row, qp_a)


def wide_kernel(mine_ref, got_ref, out_ref):
    n = mine_ref.shape[0]
    for h in range(out_ref.shape[0]):
        out_ref[h, :n] = mine_ref[...]
        out_ref[h, n:] = got_ref[...]


def widen(mine, got, n_head):
    n, blk, _ = mine.shape
    return pl.pallas_call(
        wide_kernel,
        in_specs=[VMEM_SPEC] * 2,
        out_specs=VMEM_SPEC,
        out_shape=jax.ShapeDtypeStruct((n_head, 2 * n, blk, LANES), F32),
        compiler_params=PARAMS,
        name="widen",
    )(mine, got)


def row_blocks(sc_ref, x):
    return [pl.multiple_of(128 * z + 32 * x + 16 * sc_ref[0], 16) for z in range(4)]


def query_kernel(sc_ref, step_ref, iq_ref, ik_ref, ik2_ref, w_ref, o1_ref, o2_ref, o3_ref, o0_ref, tr):
    n_head, quarters = step_ref.shape[0], step_ref.shape[1]
    jl = iq_ref.shape[1] // IDIM
    ik = jnp.concatenate([ik_ref[...], ik2_ref[...]], axis=0).astype(BF16)
    for k, out_ref in ((1, o1_ref), (2, o2_ref), (3, o3_ref), (0, o0_ref)):
        x = lax.rem(sc_ref[1] + k, 4)
        size = out_ref.shape[0]
        each = size // n_head
        start = pl.multiple_of(x * each, each)
        for c in range(quarters):
            for h in range(n_head):
                tr[pl.ds(c * size + h, each, stride=n_head), :] = step_ref[h, c, pl.ds(start, each), :]
        step = jnp.concatenate([tr[c * size : (c + 1) * size, :] for c in range(quarters)], axis=1)
        blocks = row_blocks(sc_ref, x)
        iq = jnp.concatenate([iq_ref[pl.ds(b, 16), :] for b in blocks], axis=0)
        w = jnp.concatenate([w_ref[pl.ds(b, 16), :] for b in blocks], axis=0) * INV_SCALE
        for j in range(jl):
            act = dot_t(iq[:, j * IDIM : (j + 1) * IDIM], ik)
            terms = jnp.where(act > 0.0, step * w[:, j : j + 1], 0.0).astype(BF16)
            out_ref[:, j * IDIM : (j + 1) * IDIM] = jnp.dot(terms, ik, preferred_element_type=F32)


def query_pieces(sc, step, iq, ik, ik2, w):
    n_head, quarters, half, _ = step.shape
    size = half * n_head // 4
    out = jax.ShapeDtypeStruct((size, iq.shape[1]), F32)
    return pl.pallas_call(
        query_kernel,
        in_specs=[SMEM_SPEC] + [VMEM_SPEC] * 5,
        out_specs=[VMEM_SPEC] * 4,
        out_shape=[out] * 4,
        scratch_shapes=[pltpu.VMEM((quarters * size, LANES), F32)],
        compiler_params=PARAMS,
        name="query_pieces",
    )(sc, step, iq, ik, ik2, w)


def key_kernel(sc_ref, step_ref, iq_ref, ik_ref, ik2_ref, w_ref, keep_ref, give_ref, tr, iqs, ws):
    n, quarters, half, _ = step_ref.shape
    size = n * half
    turned = []
    for c in range(quarters):
        for h in range(n):
            tr[pl.ds(h, half, stride=n), :] = step_ref[h, c]
        turned.append(tr[...].T)
    step = jnp.concatenate(turned, axis=0)
    for x in range(4):
        for z, b in enumerate(row_blocks(sc_ref, x)):
            at = 64 * x + 16 * z
            iqs[at : at + 16, :] = iq_ref[pl.ds(b, 16), :]
            ws[at : at + 16, :] = w_ref[pl.ds(b, 16), :]
    wt = ws[...].T * INV_SCALE
    ik = jnp.concatenate([ik_ref[...], ik2_ref[...]], axis=0).astype(BF16)
    total = None
    for j in range(iq_ref.shape[1] // IDIM):
        iq = iqs[:, j * IDIM : (j + 1) * IDIM]
        act = dot_t(ik, iq)
        terms = jnp.where(act > 0.0, step * wt[j : j + 1, :], 0.0).astype(BF16)
        part = jnp.dot(terms, iq, preferred_element_type=F32)
        total = part if total is None else total + part
    keys = keep_ref.shape[0]
    keep_ref[...] = total[:keys]
    give_ref[...] = total[keys:]


def key_part_grad(sc, step, iq, ik, ik2, w):
    n, _, half, _ = step.shape
    size = n * half
    out = jax.ShapeDtypeStruct(ik.shape, F32)
    return pl.pallas_call(
        key_kernel,
        in_specs=[SMEM_SPEC] + [VMEM_SPEC] * 5,
        out_specs=[VMEM_SPEC] * 2,
        out_shape=[out, out],
        scratch_shapes=[
            pltpu.VMEM((size, LANES), F32),
            pltpu.VMEM((size, iq.shape[1]), BF16),
            pltpu.VMEM((size, LANES), F32),
        ],
        compiler_params=PARAMS,
        name="key_part_grad",
    )(sc, step, iq, ik, ik2, w)


def shards(queries, attn_keys, index_queries, index_keys, head_weights, query_pos, key_offset):
    rows, keys = queries.shape[0], attn_keys.shape[0]
    n_head, n_chip = lax.axis_size(HEAD), lax.axis_size(CHIP)
    blk = rows // n_head
    hd = lax.axis_index(HEAD)
    sc = jnp.stack([lax.axis_index(a) for a in ("core", "x", "z_hi")]).astype(jnp.int32)

    key_pos = STRIDE * (lax.axis_index(CTX) * keys + jnp.arange(keys, dtype=jnp.int32)) + key_offset
    kp, qp, kp_row = key_pos[:, None], query_pos[None, :], key_pos[None, :]
    qp_a = lax.dynamic_index_in_dim(query_pos.reshape(blk, n_head), hd, 1, True)
    w_pad = jnp.pad(head_weights, ((0, 0), (0, LANES - head_weights.shape[1])))

    index, ik = part_logits(index_queries, index_keys, head_weights.T, n_head)
    index = lax.all_to_all(index, HEAD, 0, 0)
    ik2 = shift(ik, "core", 2, 1)

    lse = scores_lse(queries, attn_keys, kp, qp)
    mine, give = join_lse(sc, lse, index, kp_row, qp_a)
    mine = pair_merge(mine, shift(give, "core", 2, 1), n_chip)
    mine = merge_parts(lax.all_to_all(mine, CHIP, 0, 0))
    other = shift(mine, "core", 2, 1)
    target = probs_sum(sc, queries, attn_keys, kp, qp, mine, other, n_head)
    target = lax.all_to_all(target, HEAD, 0, 0)

    step, give = prob_step(sc, target, index, mine, kp_row, qp_a)
    step = lax.all_to_all(widen(step, shift(give, "core", 2, 1), n_head), HEAD, 0, 0)

    p1, p2, p3, own = query_pieces(sc, step, index_queries, ik, ik2, w_pad)
    own = own + shift(p1, "x", 4, 1) + shift(p2, "x", 4, 2) + shift(p3, "x", 4, 3)
    own = own.reshape(4, own.shape[0] // 4, own.shape[1])
    zi = lax.axis_index("z_hi")
    pieces = [lax.dynamic_index_in_dim(own, (zi + k) % 4, 0, False) for k in range(4)]
    query_grad = pieces[0]
    for k in range(1, 4):
        query_grad = query_grad + shift(pieces[k], "z_hi", 4, k)

    key_part, give = key_part_grad(sc, step, index_queries, ik, ik2, w_pad)
    key_part = key_part + shift(give, "core", 2, 1)
    key_part = key_part + shift(key_part, "z_lo", 2, 1)
    key_grad = key_part
    for k in range(1, 4):
        key_grad = key_grad + shift(key_part, "y", 4, k)
    return (query_grad, key_grad)


def solution(mesh):
    mesh = Mesh(mesh.devices.reshape(2, 4, 4, 4, 2), AXES)
    in_specs = (
        P(None, HEAD),
        P(CTX, HEAD),
        P(None, HEAD),
        P(CTX, None),
        P(None, HEAD),
        P(),
        P(CTX),
    )
    out_specs = (P(CTX, HEAD), P(CTX, None))
    return jax.shard_map(shards, mesh=mesh, in_specs=in_specs, out_specs=out_specs, check_vma=False)
```

```python
import math

import jax
import jax.numpy as jnp
from jax import lax
from jax.experimental import pallas as pl
from jax.experimental.pallas import tpu as pltpu
from jax.sharding import Mesh
from jax.sharding import PartitionSpec as P

HEADS = 128
HEAD_DIM = 192
IDIM = 128
STRIDE = 8
LANES = 128
NEG_FILL = -1e30
SCORE_SCALE = 1.0 / math.sqrt(HEAD_DIM)
INV_SCALE = 1.0 / math.sqrt(IDIM)

AXES = ("z_lo", "y", "z_hi", "x", "core")
HEAD = ("z_lo", "y")
CTX = ("z_hi", "x", "core")
CHIP = ("z_hi", "x")
F32, BF16 = jnp.float32, jnp.bfloat16
VMEM_SPEC = pl.BlockSpec(memory_space=pltpu.VMEM)
SMEM_SPEC = pl.BlockSpec(memory_space=pltpu.SMEM)
ANY_SPEC = pl.BlockSpec(memory_space=pl.ANY)
WIDE_PARAMS = pltpu.CompilerParams(vmem_limit_bytes=60 * 2**20)
PARAMS = pltpu.CompilerParams(vmem_limit_bytes=16 * 2**20)


def shift(value, axis, size, step):
    return lax.ppermute(value, axis, [(i, (i + step) % size) for i in range(size)])


def merge(parts):
    top = jnp.max(parts, axis=0)
    return top + jnp.log(jnp.sum(jnp.exp(parts - top[None]), axis=0))


def dot_t(a, b):
    return lax.dot_general(a, b, (((1,), (1,)), ((), ())), preferred_element_type=F32)


def head_scores(q_ref, k_ref, head):
    lane = lax.broadcasted_iota(jnp.int32, (1, LANES), 1)
    low = (lane < HEAD_DIM - LANES).astype(F32)
    at = head // 2 * 2 * HEAD_DIM + head % 2 * LANES
    q = q_ref[:, at : at + 2 * LANES]
    left, right = k_ref[:, at : at + LANES], k_ref[:, at + LANES : at + 2 * LANES]
    if head % 2 == 0:
        right = right * low.astype(BF16)
    else:
        left = left * (1.0 - low).astype(BF16)
    return dot_t(jnp.concatenate([left, right], axis=1), q) * SCORE_SCALE


def column(row, size):
    n = row.shape[1]
    wide = jnp.broadcast_to(row, (LANES, n))
    return jnp.concatenate([wide[:, i : i + LANES].T for i in range(0, n, LANES)], axis=0)


def key_positions(sc_ref, off_ref):
    keys = off_ref.shape[1]
    lane = lax.broadcasted_iota(jnp.int32, (1, keys), 1)
    return (STRIDE * (sc_ref[3] * keys + lane) + off_ref[...]).astype(F32)


def fill_bias(bias, sc_ref, off_ref, qp_ref):
    pos = column(key_positions(sc_ref, off_ref), LANES)
    for at in range(0, bias.shape[1], LANES):
        row = qp_ref[:, at : at + LANES].astype(F32)
        bias[:, at : at + LANES] = jnp.where(pos <= row, 0.0, NEG_FILL)


def split_rows(tr, out_ref, value):
    turned = value.T
    n, blk, keys = out_ref.shape
    for half in range(keys // LANES):
        span = slice(half * LANES, (half + 1) * LANES)
        tr[half * n * blk : (half + 1) * n * blk, :] = turned[:, span]
        for h in range(n):
            out_ref[h, :, span] = tr[pl.ds(half * n * blk + h, blk, stride=n), :]


def front_kernel(iq_hbm, ik_hbm, wt_hbm, out_ref, wide_ref, iq_ref, ik_ref, wt_ref, tr, sems):
    pairs = ((iq_hbm, iq_ref), (ik_hbm, ik_ref), (wt_hbm, wt_ref))
    copies = [pltpu.make_async_copy(a, b, sems.at[i]) for i, (a, b) in enumerate(pairs)]
    for copy in copies:
        copy.start()
    for copy in copies:
        copy.wait()
    total = None
    for j in range(wt_ref.shape[0]):
        act = dot_t(ik_ref[...], iq_ref[:, j * IDIM : (j + 1) * IDIM])
        term = jnp.maximum(act, 0.0) * wt_ref[j : j + 1, :]
        total = term if total is None else total + term
    split_rows(tr, out_ref, total)
    wide_ref[...] = ik_ref[...].astype(F32)


def front(iq, ik, wt, n_head):
    rows, keys = iq.shape[0], ik.shape[0]
    return pl.pallas_call(
        front_kernel,
        in_specs=[ANY_SPEC] * 3,
        out_specs=[VMEM_SPEC] * 2,
        out_shape=[
            jax.ShapeDtypeStruct((n_head, rows // n_head, keys), F32),
            jax.ShapeDtypeStruct(ik.shape, F32),
        ],
        scratch_shapes=[
            pltpu.VMEM(iq.shape, BF16),
            pltpu.VMEM(ik.shape, BF16),
            pltpu.VMEM(wt.shape, F32),
            pltpu.VMEM((rows * keys // LANES, LANES), F32),
            pltpu.SemaphoreType.DMA((3,)),
        ],
        compiler_params=WIDE_PARAMS,
        name="front",
    )(iq, ik, wt)


def lse_kernel(sc_ref, q_ref, k_ref, off_ref, qp_ref, out_ref, mask_ref, bias, tmp):
    fill_bias(bias, sc_ref, off_ref, qp_ref)
    rows, (blk, keys) = out_ref.shape[1], mask_ref.shape
    tmp[...] = column(qp_ref[...].astype(F32), LANES)
    pos_q = tmp[pl.ds(sc_ref[4], blk, stride=rows // blk), :]
    pos_k = key_positions(sc_ref, off_ref)
    for i in range(0, keys, LANES):
        mask_ref[:, i : i + LANES] = jnp.where(pos_k[:, i : i + LANES] <= pos_q, 0.0, NEG_FILL)
    for head in range(out_ref.shape[0]):
        s = head_scores(q_ref, k_ref, head) + bias[...]
        top = jnp.max(s, axis=0, keepdims=True)
        out_ref[head : head + 1, :] = top + jnp.log(jnp.sum(jnp.exp(s - top), axis=0, keepdims=True))


def scores_lse(sc, queries, attn_keys, off, qp, n_head):
    rows, keys = qp.shape[1], off.shape[1]
    heads = queries.shape[1] // HEAD_DIM
    return pl.pallas_call(
        lse_kernel,
        in_specs=[SMEM_SPEC] + [VMEM_SPEC] * 4,
        out_specs=[VMEM_SPEC] * 2,
        out_shape=[
            jax.ShapeDtypeStruct((heads, rows), F32),
            jax.ShapeDtypeStruct((rows // n_head, keys), F32),
        ],
        scratch_shapes=[pltpu.VMEM((keys, rows), F32), pltpu.VMEM((rows, LANES), F32)],
        compiler_params=PARAMS,
        name="scores_lse",
    )(sc, queries, attn_keys, off, qp)


def join_kernel(sc_ref, lse_ref, parts_ref, mask_ref, keep_ref, give_ref, logits_ref):
    half, rows = lse_ref.shape[0] // 2, lse_ref.shape[1]
    logits = jnp.sum(parts_ref[...], axis=0) * INV_SCALE + mask_ref[...]
    blk = logits.shape[0]
    logits_ref[...] = logits
    top = jnp.max(logits, axis=1, keepdims=True)
    value = top + jnp.log(jnp.sum(jnp.exp(logits - top), axis=1, keepdims=True))
    value = jnp.broadcast_to(value, (blk, LANES))
    value = jnp.concatenate([value, jnp.zeros((LANES - blk, LANES), F32)], axis=0).T
    for out_ref, core in ((keep_ref, sc_ref[0]), (give_ref, 1 - sc_ref[0])):
        out_ref[:, :rows] = lse_ref[pl.ds(pl.multiple_of(core * half, half), half), :]
        out_ref[:, rows:] = value[:half]


def join_lse(sc, lse, parts, mask):
    heads, rows = lse.shape
    out = jax.ShapeDtypeStruct((heads // 2, rows + LANES), F32)
    return pl.pallas_call(
        join_kernel,
        in_specs=[SMEM_SPEC] + [VMEM_SPEC] * 3,
        out_specs=[VMEM_SPEC] * 3,
        out_shape=[out, out, jax.ShapeDtypeStruct(mask.shape, F32)],
        compiler_params=PARAMS,
        name="join_lse",
    )(sc, lse, parts, mask)


def pair_kernel(mine_ref, got_ref, out_ref):
    both = merge(jnp.stack([mine_ref[...], got_ref[...]]))
    for c in range(out_ref.shape[0]):
        out_ref[c] = both


def pair_merge(mine, got, n_chip):
    return pl.pallas_call(
        pair_kernel,
        in_specs=[VMEM_SPEC] * 2,
        out_specs=VMEM_SPEC,
        out_shape=jax.ShapeDtypeStruct((n_chip, *mine.shape), F32),
        compiler_params=PARAMS,
        name="pair_merge",
    )(mine, got)


def merge_kernel(parts_ref, out_ref):
    out_ref[...] = merge(parts_ref[...])


def merge_parts(parts):
    return pl.pallas_call(
        merge_kernel,
        in_specs=[VMEM_SPEC],
        out_specs=VMEM_SPEC,
        out_shape=jax.ShapeDtypeStruct(parts.shape[1:], F32),
        compiler_params=PARAMS,
        name="merge_parts",
    )(parts)


def probs_kernel(
    sc_ref, q_ref, k_ref, off_ref, qp_ref, mine_ref, other_ref, b1, b2, b3, out_ref, stack_ref, bias, lse, tr
):
    fill_bias(bias, sc_ref, off_ref, qp_ref)
    half, rows = mine_ref.shape[0], lse.shape[1]
    for ref, core in ((mine_ref, sc_ref[0]), (other_ref, 1 - sc_ref[0])):
        lse[pl.ds(pl.multiple_of(core * half, half), half), :] = ref[:, :rows]
    for i, ref in enumerate((b1, b2, b3)):
        stack_ref[i] = ref[...]
    total = None
    for head in range(0, lse.shape[0], 2):
        pair = [
            jnp.exp(head_scores(q_ref, k_ref, h) + bias[...] - lse[h : h + 1, :]) for h in (head, head + 1)
        ]
        total = pair[0] + pair[1] if total is None else total + (pair[0] + pair[1])
    split_rows(tr, out_ref, total)


def probs_sum(sc, queries, attn_keys, off, qp, mine, other, blocks, n_head):
    rows, keys = qp.shape[1], off.shape[1]
    heads = queries.shape[1] // HEAD_DIM
    return pl.pallas_call(
        probs_kernel,
        in_specs=[SMEM_SPEC] + [VMEM_SPEC] * 9,
        out_specs=[VMEM_SPEC] * 2,
        out_shape=[
            jax.ShapeDtypeStruct((n_head, rows // n_head, keys), F32),
            jax.ShapeDtypeStruct((len(blocks), *blocks[0].shape), F32),
        ],
        scratch_shapes=[
            pltpu.VMEM((keys, rows), F32),
            pltpu.VMEM((heads, rows), F32),
            pltpu.VMEM((rows * keys // LANES, LANES), F32),
        ],
        compiler_params=PARAMS,
        name="probs_sum",
    )(sc, queries, attn_keys, off, qp, mine, other, *blocks)


def step_kernel(sc_ref, target_ref, logits_ref, lse_ref, keep_ref, give_ref, tmp):
    target = jnp.sum(target_ref[...], axis=0) * (1.0 / HEADS)
    blk, keys = target.shape
    rows = lse_ref.shape[1] - LANES
    lse = lse_ref[:8, rows:].T[:blk, :1]
    step = jnp.exp(logits_ref[...] - lse) - target
    for half in range(keys // LANES):
        span = slice(half * LANES, (half + 1) * LANES)
        tmp[half * blk : (half + 1) * blk, :] = step[:, span]
        for out_ref, core in ((keep_ref, sc_ref[0]), (give_ref, 1 - sc_ref[0])):
            for x in range(4):
                for r in range(2):
                    out_ref[half, pl.ds(8 * x + r, 4, stride=2), :] = tmp[
                        pl.ds(half * blk + 4 * x + 2 * core + r, 4, stride=16), :
                    ]


def prob_step(sc, target_parts, logits, lse):
    _, blk, keys = target_parts.shape
    out = jax.ShapeDtypeStruct((keys // LANES, blk // 2, LANES), F32)
    return pl.pallas_call(
        step_kernel,
        in_specs=[SMEM_SPEC] + [VMEM_SPEC] * 3,
        out_specs=[VMEM_SPEC] * 2,
        out_shape=[out, out],
        scratch_shapes=[pltpu.VMEM((blk * keys // LANES, LANES), F32)],
        compiler_params=PARAMS,
        name="prob_step",
    )(sc, target_parts, logits, lse)


def wide_kernel(sc_ref, mine_ref, got_ref, out_ref, x1_ref, x2_ref, x3_ref, x0_ref):
    n = mine_ref.shape[0]
    for h in range(out_ref.shape[0]):
        out_ref[h, :n] = mine_ref[...]
        out_ref[h, n:] = got_ref[...]
    each = x0_ref.shape[1]
    for k, x_ref in ((1, x1_ref), (2, x2_ref), (3, x3_ref), (0, x0_ref)):
        rows = pl.ds(pl.multiple_of(lax.rem(sc_ref[1] + k, 4) * each, each), each)
        x_ref[:n] = mine_ref[:, rows, :]
        x_ref[n:] = got_ref[:, rows, :]


def widen(sc, mine, got, n_head):
    n, half, _ = mine.shape
    piece = jax.ShapeDtypeStruct((2 * n, half // 4, LANES), F32)
    return pl.pallas_call(
        wide_kernel,
        in_specs=[SMEM_SPEC] + [VMEM_SPEC] * 2,
        out_specs=[VMEM_SPEC] * 5,
        out_shape=[jax.ShapeDtypeStruct((n_head, 2 * n, half, LANES), F32)] + [piece] * 4,
        compiler_params=PARAMS,
        name="widen",
    )(sc, mine, got)


def around_kernel(p0, p1, p2, p3, out_ref):
    for h in range(out_ref.shape[0]):
        for k, ref in enumerate((p0, p1, p2, p3)):
            out_ref[h, k] = ref[...]


def repeat_parts(parts, n_head):
    return pl.pallas_call(
        around_kernel,
        in_specs=[VMEM_SPEC] * 4,
        out_specs=VMEM_SPEC,
        out_shape=jax.ShapeDtypeStruct((n_head, len(parts), *parts[0].shape), F32),
        compiler_params=PARAMS,
        name="repeat_parts",
    )(*parts)


def weight_rows(wt_ref):
    wt = wt_ref[...] * INV_SCALE
    return jnp.concatenate([wt, jnp.zeros((LANES - wt.shape[0], wt.shape[1]), F32)], axis=0).T


def row_blocks(sc_ref, x):
    return [pl.multiple_of(128 * z + 32 * x + 16 * sc_ref[0], 16) for z in range(4)]


def query_kernel(sc_ref, step_ref, iq_ref, wt_ref, ik_ref, ik2_ref, own_ref, far_ref, o1_ref, o2_ref, o3_ref, o0_ref, tr, iqs, acc, w_ref):
    w_ref[...] = weight_rows(wt_ref)
    n_head, n_x, quarters, each, _ = step_ref.shape
    size = each * n_head
    jl = iq_ref.shape[1] // IDIM
    blocks = row_blocks(sc_ref, sc_ref[1])
    w = jnp.concatenate([w_ref[pl.ds(b, 16), :] for b in blocks], axis=0)
    for j in range(jl):
        for z, b in enumerate(blocks):
            iqs[j * size + 16 * z : j * size + 16 * z + 16, :] = iq_ref[pl.ds(b, 16), j * IDIM : (j + 1) * IDIM]
    total = None
    for k in range(n_x):
        for c in range(quarters):
            for h in range(n_head):
                at = (k * quarters + c) * size
                tr[pl.ds(at + h, each, stride=n_head), :] = step_ref[h, k, c]
        step = jnp.concatenate(
            [tr[(k * quarters + c) * size : (k * quarters + c + 1) * size, :] for c in range(quarters)], axis=1
        )
        near, far = (ik_ref[...], ik2_ref[...]) if k == 0 else (own_ref[k - 1], far_ref[k - 1])
        ik = jnp.concatenate([near, far], axis=0).astype(BF16)
        act = dot_t(iqs[...], ik)
        terms = jnp.concatenate(
            [
                jnp.where(act[j * size : (j + 1) * size] > 0.0, step * w[:, j : j + 1], 0.0).astype(BF16)
                for j in range(jl)
            ],
            axis=0,
        )
        part = jnp.dot(terms, ik, preferred_element_type=F32)
        total = part if total is None else total + part
    acc[...] = total
    piece = size // 4
    for k, out_ref in ((1, o1_ref), (2, o2_ref), (3, o3_ref), (0, o0_ref)):
        z = lax.rem(sc_ref[2] + k, 4)
        for j in range(jl):
            out_ref[:, j * IDIM : (j + 1) * IDIM] = acc[pl.ds(pl.multiple_of(j * size + z * piece, piece), piece), :]


def query_pieces(sc, step, iq, wt, ik, ik2, own, far):
    n_head, n_x, quarters, each, _ = step.shape
    size = each * n_head
    out = jax.ShapeDtypeStruct((size // 4, iq.shape[1]), F32)
    return pl.pallas_call(
        query_kernel,
        in_specs=[SMEM_SPEC] + [VMEM_SPEC] * 7,
        out_specs=[VMEM_SPEC] * 4,
        out_shape=[out] * 4,
        scratch_shapes=[
            pltpu.VMEM((n_x * quarters * size, LANES), F32),
            pltpu.VMEM((size * iq.shape[1] // IDIM, IDIM), BF16),
            pltpu.VMEM((size * iq.shape[1] // IDIM, IDIM), F32),
            pltpu.VMEM((iq.shape[0], LANES), F32),
        ],
        compiler_params=PARAMS,
        name="query_pieces",
    )(sc, step, iq, wt, ik, ik2, own, far)


def key_kernel(sc_ref, step_ref, iq_ref, ik_ref, ik2_ref, wt_ref, keep_ref, give_ref, tr, iqs, ws, w_ref):
    w_ref[...] = weight_rows(wt_ref)
    n, quarters, half, _ = step_ref.shape
    size = n * half
    turned = []
    for c in range(quarters):
        for h in range(n):
            tr[pl.ds(h, half, stride=n), :] = step_ref[h, c]
        turned.append(tr[...].T)
    step = jnp.concatenate(turned, axis=0)
    for x in range(4):
        for z, b in enumerate(row_blocks(sc_ref, x)):
            at = 64 * x + 16 * z
            iqs[at : at + 16, :] = iq_ref[pl.ds(b, 16), :]
            ws[at : at + 16, :] = w_ref[pl.ds(b, 16), :]
    wt = ws[...].T
    ik = jnp.concatenate([ik_ref[...], ik2_ref[...]], axis=0).astype(BF16)
    total = None
    for j in range(iq_ref.shape[1] // IDIM):
        iq = iqs[:, j * IDIM : (j + 1) * IDIM]
        act = dot_t(ik, iq)
        terms = jnp.where(act > 0.0, step * wt[j : j + 1, :], 0.0).astype(BF16)
        part = jnp.dot(terms, iq, preferred_element_type=F32)
        total = part if total is None else total + part
    keys = keep_ref.shape[0]
    keep_ref[...] = total[:keys]
    give_ref[...] = total[keys:]


def key_part_grad(sc, step, iq, ik, ik2, wt):
    n, _, half, _ = step.shape
    size = n * half
    out = jax.ShapeDtypeStruct(ik.shape, F32)
    return pl.pallas_call(
        key_kernel,
        in_specs=[SMEM_SPEC] + [VMEM_SPEC] * 5,
        out_specs=[VMEM_SPEC] * 2,
        out_shape=[out, out],
        scratch_shapes=[
            pltpu.VMEM((size, LANES), F32),
            pltpu.VMEM((size, iq.shape[1]), BF16),
            pltpu.VMEM((size, LANES), F32),
            pltpu.VMEM((iq.shape[0], LANES), F32),
        ],
        compiler_params=PARAMS,
        name="key_part_grad",
    )(sc, step, iq, ik, ik2, wt)


def shards(queries, attn_keys, index_queries, index_keys, head_weights, query_pos, key_offset):
    n_head, n_chip = lax.axis_size(HEAD), lax.axis_size(CHIP)
    sc = jnp.stack([lax.axis_index(a) for a in ("core", "x", "z_hi", CTX, HEAD)]).astype(jnp.int32)

    off, qp = key_offset[None, :], query_pos[None, :]
    w_t = head_weights.T

    index, ik = front(index_queries, index_keys, w_t, n_head)
    index = lax.all_to_all(index, HEAD, 0, 0)
    ik2 = shift(ik, "core", 2, 1)

    lse, mask = scores_lse(sc, queries, attn_keys, off, qp, n_head)
    mine, give, logits = join_lse(sc, lse, index, mask)
    mine = pair_merge(mine, shift(give, "core", 2, 1), n_chip)
    mine = merge_parts(lax.all_to_all(mine, CHIP, 0, 0))
    other = shift(mine, "core", 2, 1)
    around = [shift(ik, "x", 4, k) for k in range(1, 4)]
    target, around = probs_sum(sc, queries, attn_keys, off, qp, mine, other, around, n_head)
    target = lax.all_to_all(target, HEAD, 0, 0)

    step, give = prob_step(sc, target, logits, mine)
    step_key, *pieces = widen(sc, step, shift(give, "core", 2, 1), n_head)
    step_key = lax.all_to_all(step_key, HEAD, 0, 0)
    pieces = [pieces[3]] + [shift(pieces[k - 1], "x", 4, k) for k in range(1, 4)]
    step_query = lax.all_to_all(repeat_parts(pieces, n_head), HEAD, 0, 0)

    p1, p2, p3, query_grad = query_pieces(
        sc, step_query, index_queries, w_t, ik, ik2, around, shift(around, "core", 2, 1)
    )
    query_grad = query_grad + shift(p1, "z_hi", 4, 1) + shift(p2, "z_hi", 4, 2) + shift(p3, "z_hi", 4, 3)

    key_part, give = key_part_grad(sc, step_key, index_queries, ik, ik2, w_t)
    key_part = key_part + shift(give, "core", 2, 1)
    key_part = key_part + shift(key_part, "z_lo", 2, 1)
    key_grad = key_part
    for k in range(1, 4):
        key_grad = key_grad + shift(key_part, "y", 4, k)
    return (query_grad, key_grad)


def solution(mesh):
    mesh = Mesh(mesh.devices.reshape(2, 4, 4, 4, 2), AXES)
    in_specs = (
        P(None, HEAD),
        P(CTX, HEAD),
        P(None, HEAD),
        P(CTX, None),
        P(None, HEAD),
        P(),
        P(CTX),
    )
    out_specs = (P(CTX, HEAD), P(CTX, None))
    return jax.shard_map(shards, mesh=mesh, in_specs=in_specs, out_specs=out_specs, check_vma=False)
```

```python
import math

import jax
import jax.numpy as jnp
from jax import lax
from jax.experimental import pallas as pl
from jax.experimental.pallas import tpu as pltpu
from jax.sharding import Mesh
from jax.sharding import PartitionSpec as P

HEADS = 128
HEAD_DIM = 192
IDIM = 128
STRIDE = 8
LANES = 128
NEG_FILL = -1e30
SCORE_SCALE = 1.0 / math.sqrt(HEAD_DIM)
INV_SCALE = 1.0 / math.sqrt(IDIM)

AXES = ("z_lo", "y", "z_hi", "x", "core")
HEAD = ("z_lo", "y")
CTX = ("z_hi", "x", "core")
CHIP = ("z_hi", "x")
F32, BF16 = jnp.float32, jnp.bfloat16
VMEM_SPEC = pl.BlockSpec(memory_space=pltpu.VMEM)
SMEM_SPEC = pl.BlockSpec(memory_space=pltpu.SMEM)
ANY_SPEC = pl.BlockSpec(memory_space=pl.ANY)
WIDE_PARAMS = pltpu.CompilerParams(vmem_limit_bytes=60 * 2**20)
PARAMS = pltpu.CompilerParams(vmem_limit_bytes=16 * 2**20)


def shift(value, axis, size, step):
    return lax.ppermute(value, axis, [(i, (i + step) % size) for i in range(size)])


def merge(parts):
    top = jnp.max(parts, axis=0)
    return top + jnp.log(jnp.sum(jnp.exp(parts - top[None]), axis=0))


def dot_t(a, b):
    return lax.dot_general(a, b, (((1,), (1,)), ((), ())), preferred_element_type=F32)


def head_scores(q_ref, k_ref, head):
    lane = lax.broadcasted_iota(jnp.int32, (1, LANES), 1)
    low = (lane < HEAD_DIM - LANES).astype(F32)
    at = head // 2 * 2 * HEAD_DIM + head % 2 * LANES
    q = q_ref[:, at : at + 2 * LANES]
    left, right = k_ref[:, at : at + LANES], k_ref[:, at + LANES : at + 2 * LANES]
    if head % 2 == 0:
        right = right * low.astype(BF16)
    else:
        left = left * (1.0 - low).astype(BF16)
    return dot_t(jnp.concatenate([left, right], axis=1), q) * SCORE_SCALE


def column(row, size):
    n = row.shape[1]
    wide = jnp.broadcast_to(row, (LANES, n))
    return jnp.concatenate([wide[:, i : i + LANES].T for i in range(0, n, LANES)], axis=0)


def key_positions(sc_ref, off_ref):
    keys = off_ref.shape[1]
    lane = lax.broadcasted_iota(jnp.int32, (1, keys), 1)
    return (STRIDE * (sc_ref[3] * keys + lane) + off_ref[...]).astype(F32)


def fill_bias(bias, sc_ref, off_ref, qp_ref):
    pos = column(key_positions(sc_ref, off_ref), LANES)
    for at in range(0, bias.shape[1], LANES):
        row = qp_ref[:, at : at + LANES].astype(F32)
        bias[:, at : at + LANES] = jnp.where(pos <= row, 0.0, NEG_FILL)


def split_rows(tr, out_ref, value):
    turned = value.T
    n, blk, keys = out_ref.shape
    for half in range(keys // LANES):
        span = slice(half * LANES, (half + 1) * LANES)
        tr[half * n * blk : (half + 1) * n * blk, :] = turned[:, span]
        for h in range(n):
            out_ref[h, :, span] = tr[pl.ds(half * n * blk + h, blk, stride=n), :]


def front_kernel(iq_hbm, ik_hbm, wt_hbm, out_ref, wide_ref, iq_ref, ik_ref, wt_ref, tr, sems):
    pairs = ((iq_hbm, iq_ref), (ik_hbm, ik_ref), (wt_hbm, wt_ref))
    copies = [pltpu.make_async_copy(a, b, sems.at[i]) for i, (a, b) in enumerate(pairs)]
    for copy in copies:
        copy.start()
    for copy in copies:
        copy.wait()
    total = None
    for j in range(wt_ref.shape[0]):
        act = dot_t(ik_ref[...], iq_ref[:, j * IDIM : (j + 1) * IDIM])
        term = jnp.maximum(act, 0.0) * wt_ref[j : j + 1, :]
        total = term if total is None else total + term
    split_rows(tr, out_ref, total)
    wide_ref[...] = ik_ref[...].astype(F32)


def front(iq, ik, wt, n_head):
    rows, keys = iq.shape[0], ik.shape[0]
    return pl.pallas_call(
        front_kernel,
        in_specs=[ANY_SPEC] * 3,
        out_specs=[VMEM_SPEC] * 2,
        out_shape=[
            jax.ShapeDtypeStruct((n_head, rows // n_head, keys), F32),
            jax.ShapeDtypeStruct(ik.shape, F32),
        ],
        scratch_shapes=[
            pltpu.VMEM(iq.shape, BF16),
            pltpu.VMEM(ik.shape, BF16),
            pltpu.VMEM(wt.shape, F32),
            pltpu.VMEM((rows * keys // LANES, LANES), F32),
            pltpu.SemaphoreType.DMA((3,)),
        ],
        compiler_params=WIDE_PARAMS,
        name="front",
    )(iq, ik, wt)


def lse_kernel(sc_ref, q_ref, k_ref, off_ref, qp_ref, out_ref, mask_ref, bias, tmp):
    fill_bias(bias, sc_ref, off_ref, qp_ref)
    rows, (blk, keys) = out_ref.shape[1], mask_ref.shape
    tmp[...] = column(qp_ref[...].astype(F32), LANES)
    pos_q = tmp[pl.ds(sc_ref[4], blk, stride=rows // blk), :]
    pos_k = key_positions(sc_ref, off_ref)
    for i in range(0, keys, LANES):
        mask_ref[:, i : i + LANES] = jnp.where(pos_k[:, i : i + LANES] <= pos_q, 0.0, NEG_FILL)
    for head in range(out_ref.shape[0]):
        s = head_scores(q_ref, k_ref, head) + bias[...]
        top = jnp.max(s, axis=0, keepdims=True)
        out_ref[head : head + 1, :] = top + jnp.log(jnp.sum(jnp.exp(s - top), axis=0, keepdims=True))


def scores_lse(sc, queries, attn_keys, off, qp, n_head):
    rows, keys = qp.shape[1], off.shape[1]
    heads = queries.shape[1] // HEAD_DIM
    return pl.pallas_call(
        lse_kernel,
        in_specs=[SMEM_SPEC] + [VMEM_SPEC] * 4,
        out_specs=[VMEM_SPEC] * 2,
        out_shape=[
            jax.ShapeDtypeStruct((heads, rows), F32),
            jax.ShapeDtypeStruct((rows // n_head, keys), F32),
        ],
        scratch_shapes=[pltpu.VMEM((keys, rows), F32), pltpu.VMEM((rows, LANES), F32)],
        compiler_params=PARAMS,
        name="scores_lse",
    )(sc, queries, attn_keys, off, qp)


def join_kernel(sc_ref, lse_ref, parts_ref, mask_ref, keep_ref, give_ref, logits_ref):
    half, rows = lse_ref.shape[0] // 2, lse_ref.shape[1]
    logits = jnp.sum(parts_ref[...], axis=0) * INV_SCALE + mask_ref[...]
    blk = logits.shape[0]
    logits_ref[...] = logits
    top = jnp.max(logits, axis=1, keepdims=True)
    value = top + jnp.log(jnp.sum(jnp.exp(logits - top), axis=1, keepdims=True))
    value = jnp.broadcast_to(value, (blk, LANES))
    value = jnp.concatenate([value, jnp.zeros((LANES - blk, LANES), F32)], axis=0).T
    for out_ref, core in ((keep_ref, sc_ref[0]), (give_ref, 1 - sc_ref[0])):
        out_ref[:, :rows] = lse_ref[pl.ds(pl.multiple_of(core * half, half), half), :]
        out_ref[:, rows:] = value[:half]


def join_lse(sc, lse, parts, mask):
    heads, rows = lse.shape
    out = jax.ShapeDtypeStruct((heads // 2, rows + LANES), F32)
    return pl.pallas_call(
        join_kernel,
        in_specs=[SMEM_SPEC] + [VMEM_SPEC] * 3,
        out_specs=[VMEM_SPEC] * 3,
        out_shape=[out, out, jax.ShapeDtypeStruct(mask.shape, F32)],
        compiler_params=PARAMS,
        name="join_lse",
    )(sc, lse, parts, mask)


def pair_kernel(mine_ref, got_ref, out_ref):
    both = merge(jnp.stack([mine_ref[...], got_ref[...]]))
    for c in range(out_ref.shape[0]):
        out_ref[c] = both


def pair_merge(mine, got, n_chip):
    return pl.pallas_call(
        pair_kernel,
        in_specs=[VMEM_SPEC] * 2,
        out_specs=VMEM_SPEC,
        out_shape=jax.ShapeDtypeStruct((n_chip, *mine.shape), F32),
        compiler_params=PARAMS,
        name="pair_merge",
    )(mine, got)


def merge_kernel(parts_ref, out_ref):
    out_ref[...] = merge(parts_ref[...])


def merge_parts(parts):
    return pl.pallas_call(
        merge_kernel,
        in_specs=[VMEM_SPEC],
        out_specs=VMEM_SPEC,
        out_shape=jax.ShapeDtypeStruct(parts.shape[1:], F32),
        compiler_params=PARAMS,
        name="merge_parts",
    )(parts)


def probs_kernel(
    sc_ref, q_ref, k_ref, off_ref, qp_ref, mine_ref, other_ref, b1, b2, b3, out_ref, bias, lse, tr
):
    fill_bias(bias, sc_ref, off_ref, qp_ref)
    half, rows = mine_ref.shape[0], lse.shape[1]
    for ref, core in ((mine_ref, sc_ref[0]), (other_ref, 1 - sc_ref[0])):
        lse[pl.ds(pl.multiple_of(core * half, half), half), :] = ref[:, :rows]
    total = None
    for head in range(0, lse.shape[0], 2):
        pair = [
            jnp.exp(head_scores(q_ref, k_ref, h) + bias[...] - lse[h : h + 1, :]) for h in (head, head + 1)
        ]
        total = pair[0] + pair[1] if total is None else total + (pair[0] + pair[1])
    split_rows(tr, out_ref, total)


def probs_sum(sc, queries, attn_keys, off, qp, mine, other, blocks, n_head):
    rows, keys = qp.shape[1], off.shape[1]
    heads = queries.shape[1] // HEAD_DIM
    return pl.pallas_call(
        probs_kernel,
        in_specs=[SMEM_SPEC] + [VMEM_SPEC] * 6 + [ANY_SPEC] * 3,
        out_specs=VMEM_SPEC,
        out_shape=jax.ShapeDtypeStruct((n_head, rows // n_head, keys), F32),
        scratch_shapes=[
            pltpu.VMEM((keys, rows), F32),
            pltpu.VMEM((heads, rows), F32),
            pltpu.VMEM((rows * keys // LANES, LANES), F32),
        ],
        compiler_params=PARAMS,
        name="probs_sum",
    )(sc, queries, attn_keys, off, qp, mine, other, *blocks)


def step_kernel(sc_ref, target_ref, logits_ref, lse_ref, wide_ref, x1_ref, x2_ref, x3_ref, x0_ref, tmp, turn):
    target = jnp.sum(target_ref[...], axis=0) * (1.0 / HEADS)
    blk, keys = target.shape
    rows = lse_ref.shape[1] - LANES
    lse = lse_ref[:8, rows:].T[:blk, :1]
    step = jnp.exp(logits_ref[...] - lse) - target
    for half in range(keys // LANES):
        part = step[:, half * LANES : (half + 1) * LANES]
        for h in range(wide_ref.shape[0]):
            wide_ref[h, half] = part
        tmp[half] = part
        for z in range(4):
            for x in range(4):
                turn[half, 16 * x + 4 * z : 16 * x + 4 * z + 4, :] = tmp[half, 16 * z + 4 * x : 16 * z + 4 * x + 4, :]
    for k, x_ref in ((1, x1_ref), (2, x2_ref), (3, x3_ref), (0, x0_ref)):
        x_ref[...] = turn[:, pl.ds(pl.multiple_of(lax.rem(sc_ref[1] + k, 4) * 16, 16), 16), :]


def prob_step(sc, target_parts, logits, lse):
    n_head, blk, keys = target_parts.shape
    halves = keys // LANES
    piece = jax.ShapeDtypeStruct((halves, blk // 4, LANES), F32)
    return pl.pallas_call(
        step_kernel,
        in_specs=[SMEM_SPEC] + [VMEM_SPEC] * 3,
        out_specs=[VMEM_SPEC] * 5,
        out_shape=[jax.ShapeDtypeStruct((n_head, halves, blk, LANES), F32)] + [piece] * 4,
        scratch_shapes=[pltpu.VMEM((halves, blk, LANES), F32)] * 2,
        compiler_params=PARAMS,
        name="prob_step",
    )(sc, target_parts, logits, lse)


def around_kernel(p0, p1, p2, p3, first, out_ref):
    for h in range(out_ref.shape[0]):
        for k, ref in enumerate((p0, p1, p2, p3)):
            out_ref[h, k] = ref[...]


def repeat_parts(parts, first, n_head):
    return pl.pallas_call(
        around_kernel,
        in_specs=[VMEM_SPEC] * 4 + [ANY_SPEC],
        out_specs=VMEM_SPEC,
        out_shape=jax.ShapeDtypeStruct((n_head, len(parts), *parts[0].shape), F32),
        compiler_params=PARAMS,
        name="repeat_parts",
    )(*parts, first)


def weight_rows(wt_ref):
    wt = wt_ref[...] * INV_SCALE
    return jnp.concatenate([wt, jnp.zeros((LANES - wt.shape[0], wt.shape[1]), F32)], axis=0).T


def query_kernel(sc_ref, step_ref, iq_ref, wt_ref, i0_ref, i1_ref, i2_ref, i3_ref, first, keep_ref, give_ref, tr, iqs, acc, w_ref):
    w_ref[...] = weight_rows(wt_ref)
    n_head, n_x, quarters, each, _ = step_ref.shape
    size = each * n_head
    block = size // 4
    jl = iq_ref.shape[1] // IDIM
    starts = [pl.multiple_of(4 * block * z + block * sc_ref[1], block) for z in range(4)]
    w = jnp.concatenate([w_ref[pl.ds(b, block), :] for b in starts], axis=0)
    for j in range(jl):
        for z, b in enumerate(starts):
            at = j * size + block * z
            iqs[at : at + block, :] = iq_ref[pl.ds(b, block), j * IDIM : (j + 1) * IDIM]
    total = None
    for k, ik_ref in enumerate((i0_ref, i1_ref, i2_ref, i3_ref)):
        for c in range(quarters):
            for h in range(n_head):
                tr[pl.ds((k * quarters + c) * size + h, each, stride=n_head), :] = step_ref[h, k, c]
        step = jnp.concatenate(
            [tr[(k * quarters + c) * size : (k * quarters + c + 1) * size, :] for c in range(quarters)], axis=1
        )
        ik = ik_ref[...].astype(BF16)
        act = dot_t(iqs[...], ik)
        terms = jnp.concatenate(
            [
                jnp.where(act[j * size : (j + 1) * size] > 0.0, step * w[:, j : j + 1], 0.0).astype(BF16)
                for j in range(jl)
            ],
            axis=0,
        )
        part = jnp.dot(terms, ik, preferred_element_type=F32)
        total = part if total is None else total + part
    acc[...] = total
    piece = block // 2
    for out_ref, core in ((give_ref, 1 - sc_ref[0]), (keep_ref, sc_ref[0])):
        for i, k in enumerate((1, 2, 3, 0)):
            z = lax.rem(sc_ref[2] + k, 4)
            for j in range(jl):
                at = pl.multiple_of(j * size + z * block + core * piece, piece)
                out_ref[i * piece : (i + 1) * piece, j * IDIM : (j + 1) * IDIM] = acc[pl.ds(at, piece), :]


def query_pieces(sc, step, iq, wt, blocks, first):
    n_head, n_x, quarters, each, _ = step.shape
    size = each * n_head
    jl = iq.shape[1] // IDIM
    out = jax.ShapeDtypeStruct((size // 2, iq.shape[1]), F32)
    return pl.pallas_call(
        query_kernel,
        in_specs=[SMEM_SPEC] + [VMEM_SPEC] * 7 + [ANY_SPEC],
        out_specs=[VMEM_SPEC] * 2,
        out_shape=[out] * 2,
        scratch_shapes=[
            pltpu.VMEM((n_x * quarters * size, LANES), F32),
            pltpu.VMEM((size * jl, IDIM), BF16),
            pltpu.VMEM((size * jl, IDIM), F32),
            pltpu.VMEM((iq.shape[0], LANES), F32),
        ],
        compiler_params=PARAMS,
        name="query_pieces",
    )(sc, step, iq, wt, *blocks, first)


def fold_kernel(keep_ref, got_ref, o1_ref, o2_ref, o3_ref, o0_ref):
    piece = o0_ref.shape[0]
    for i, out_ref in enumerate((o1_ref, o2_ref, o3_ref, o0_ref)):
        out_ref[...] = keep_ref[i * piece : (i + 1) * piece] + got_ref[i * piece : (i + 1) * piece]


def fold(keep, got):
    out = jax.ShapeDtypeStruct((keep.shape[0] // 4, keep.shape[1]), F32)
    return pl.pallas_call(
        fold_kernel,
        in_specs=[VMEM_SPEC] * 2,
        out_specs=[VMEM_SPEC] * 4,
        out_shape=[out] * 4,
        compiler_params=PARAMS,
        name="fold",
    )(keep, got)


def key_kernel(step_ref, iq_ref, ik_ref, wt_ref, out_ref, tr):
    n, halves, blk, _ = step_ref.shape
    turned = []
    for c in range(halves):
        base = c * n * blk
        for h in range(n):
            tr[pl.ds(base + h, blk, stride=n), :] = step_ref[h, c]
        turned.append(tr[base : base + n * blk, :].T)
    step = jnp.concatenate(turned, axis=0)
    ik = ik_ref[...].astype(BF16)
    total = None
    for j in range(wt_ref.shape[0]):
        iq = iq_ref[:, j * IDIM : (j + 1) * IDIM]
        act = dot_t(ik, iq)
        terms = jnp.where(act > 0.0, step * (wt_ref[j : j + 1, :] * INV_SCALE), 0.0).astype(BF16)
        part = jnp.dot(terms, iq, preferred_element_type=F32)
        total = part if total is None else total + part
    out_ref[...] = total


def key_part_grad(step, iq, ik, wt):
    n, halves, blk, _ = step.shape
    return pl.pallas_call(
        key_kernel,
        in_specs=[VMEM_SPEC] * 4,
        out_specs=VMEM_SPEC,
        out_shape=jax.ShapeDtypeStruct(ik.shape, F32),
        scratch_shapes=[pltpu.VMEM((n * halves * blk, LANES), F32)],
        compiler_params=PARAMS,
        name="key_part_grad",
    )(step, iq, ik, wt)


def shards(queries, attn_keys, index_queries, index_keys, head_weights, query_pos, key_offset):
    n_head, n_chip = lax.axis_size(HEAD), lax.axis_size(CHIP)
    sc = jnp.stack([lax.axis_index(a) for a in ("core", "x", "z_hi", CTX, HEAD)]).astype(jnp.int32)

    off, qp = key_offset[None, :], query_pos[None, :]
    w_t = head_weights.T

    index, ik = front(index_queries, index_keys, w_t, n_head)
    index = lax.all_to_all(index, HEAD, 0, 0)

    lse, mask = scores_lse(sc, queries, attn_keys, off, qp, n_head)
    mine, give, logits = join_lse(sc, lse, index, mask)
    mine = pair_merge(mine, shift(give, "core", 2, 1), n_chip)
    mine = merge_parts(lax.all_to_all(mine, CHIP, 0, 0))
    other = shift(mine, "core", 2, 1)
    around = [shift(ik, "x", 4, k) for k in range(1, 4)]
    target = probs_sum(sc, queries, attn_keys, off, qp, mine, other, around, n_head)
    target = lax.all_to_all(target, HEAD, 0, 0)

    step_key, *pieces = prob_step(sc, target, logits, mine)
    step_key = lax.all_to_all(step_key, HEAD, 0, 0)
    pieces = [pieces[3]] + [shift(pieces[k - 1], "x", 4, k) for k in range(1, 4)]
    step_query = lax.all_to_all(repeat_parts(pieces, step_key, n_head), HEAD, 0, 0)

    key_part = key_part_grad(step_key, index_queries, ik, w_t)
    key_part = key_part + shift(key_part, "z_lo", 2, 1)
    key_grad = key_part
    for k in range(1, 4):
        key_grad = key_grad + shift(key_part, "y", 4, k)

    keep, give = query_pieces(sc, step_query, index_queries, w_t, [ik] + around, key_part)
    p1, p2, p3, query_grad = fold(keep, shift(give, "core", 2, 1))
    query_grad = query_grad + shift(p1, "z_hi", 4, 1) + shift(p2, "z_hi", 4, 2) + shift(p3, "z_hi", 4, 3)
    return (query_grad, key_grad)


def solution(mesh):
    mesh = Mesh(mesh.devices.reshape(2, 4, 4, 4, 2), AXES)
    in_specs = (
        P(None, HEAD),
        P(CTX, HEAD),
        P(None, HEAD),
        P(CTX, None),
        P(None, HEAD),
        P(),
        P(CTX),
    )
    out_specs = (P(CTX, HEAD), P(CTX, None))
    return jax.shard_map(shards, mesh=mesh, in_specs=in_specs, out_specs=out_specs, check_vma=False)
```

```python
import math

import jax
import jax.numpy as jnp
from jax import lax
from jax.experimental import pallas as pl
from jax.experimental.pallas import tpu as pltpu
from jax.sharding import Mesh
from jax.sharding import PartitionSpec as P

HEADS = 128
HEAD_DIM = 192
IDIM = 128
STRIDE = 8
LANES = 128
NEG_FILL = -1e30
SCORE_SCALE = 1.0 / math.sqrt(HEAD_DIM)
INV_SCALE = 1.0 / math.sqrt(IDIM)

AXES = ("z_lo", "y", "z_hi", "x", "core")
HEAD = ("z_lo", "y")
CTX = ("z_hi", "x", "core")
CHIP = ("z_hi", "x")
F32, BF16 = jnp.float32, jnp.bfloat16
VMEM_SPEC = pl.BlockSpec(memory_space=pltpu.VMEM)
SMEM_SPEC = pl.BlockSpec(memory_space=pltpu.SMEM)
ANY_SPEC = pl.BlockSpec(memory_space=pl.ANY)
WIDE_PARAMS = pltpu.CompilerParams(vmem_limit_bytes=60 * 2**20)
PARAMS = pltpu.CompilerParams(vmem_limit_bytes=16 * 2**20)


def shift(value, axis, size, step):
    return lax.ppermute(value, axis, [(i, (i + step) % size) for i in range(size)])


def merge(parts):
    top = jnp.max(parts, axis=0)
    return top + jnp.log(jnp.sum(jnp.exp(parts - top[None]), axis=0))


def dot_t(a, b):
    return lax.dot_general(a, b, (((1,), (1,)), ((), ())), preferred_element_type=F32)


def head_scores(q_ref, k_ref, head):
    lane = lax.broadcasted_iota(jnp.int32, (1, LANES), 1)
    low = (lane < HEAD_DIM - LANES).astype(F32)
    at = head // 2 * 2 * HEAD_DIM + head % 2 * LANES
    q = q_ref[:, at : at + 2 * LANES]
    left, right = k_ref[:, at : at + LANES], k_ref[:, at + LANES : at + 2 * LANES]
    if head % 2 == 0:
        right = right * low.astype(BF16)
    else:
        left = left * (1.0 - low).astype(BF16)
    return dot_t(jnp.concatenate([left, right], axis=1), q) * SCORE_SCALE


def column(row, size):
    n = row.shape[1]
    wide = jnp.broadcast_to(row, (LANES, n))
    return jnp.concatenate([wide[:, i : i + LANES].T for i in range(0, n, LANES)], axis=0)


def key_positions(sc_ref, off_ref):
    keys = off_ref.shape[1]
    lane = lax.broadcasted_iota(jnp.int32, (1, keys), 1)
    return (STRIDE * (sc_ref[3] * keys + lane) + off_ref[...]).astype(F32)


def fill_bias(bias, sc_ref, off_ref, qp_ref):
    pos = column(key_positions(sc_ref, off_ref), LANES)
    for at in range(0, bias.shape[1], LANES):
        row = qp_ref[:, at : at + LANES].astype(F32)
        bias[:, at : at + LANES] = jnp.where(pos <= row, 0.0, NEG_FILL)


def split_rows(tr, out_ref, value):
    turned = value.T
    n, blk, keys = out_ref.shape
    for half in range(keys // LANES):
        span = slice(half * LANES, (half + 1) * LANES)
        tr[half * n * blk : (half + 1) * n * blk, :] = turned[:, span]
        for h in range(n):
            out_ref[h, :, span] = tr[pl.ds(half * n * blk + h, blk, stride=n), :]


def front_kernel(iq_hbm, ik_hbm, wt_hbm, out_ref, wide_ref, iq_ref, ik_ref, wt_ref, tr, sems):
    pairs = ((iq_hbm, iq_ref), (ik_hbm, ik_ref), (wt_hbm, wt_ref))
    copies = [pltpu.make_async_copy(a, b, sems.at[i]) for i, (a, b) in enumerate(pairs)]
    for copy in copies:
        copy.start()
    for copy in copies:
        copy.wait()
    total = None
    for j in range(wt_ref.shape[0]):
        act = dot_t(ik_ref[...], iq_ref[:, j * IDIM : (j + 1) * IDIM])
        term = jnp.maximum(act, 0.0) * wt_ref[j : j + 1, :]
        total = term if total is None else total + term
    split_rows(tr, out_ref, total)
    wide_ref[...] = ik_ref[...].astype(F32)


def front(iq, ik, wt, n_head):
    rows, keys = iq.shape[0], ik.shape[0]
    return pl.pallas_call(
        front_kernel,
        in_specs=[ANY_SPEC] * 3,
        out_specs=[VMEM_SPEC] * 2,
        out_shape=[
            jax.ShapeDtypeStruct((n_head, rows // n_head, keys), F32),
            jax.ShapeDtypeStruct(ik.shape, F32),
        ],
        scratch_shapes=[
            pltpu.VMEM(iq.shape, BF16),
            pltpu.VMEM(ik.shape, BF16),
            pltpu.VMEM(wt.shape, F32),
            pltpu.VMEM((rows * keys // LANES, LANES), F32),
            pltpu.SemaphoreType.DMA((3,)),
        ],
        compiler_params=WIDE_PARAMS,
        name="front",
    )(iq, ik, wt)


def lse_kernel(sc_ref, q_ref, k_ref, off_ref, qp_ref, out_ref, mask_ref, bias, tmp):
    fill_bias(bias, sc_ref, off_ref, qp_ref)
    rows, (blk, keys) = out_ref.shape[1], mask_ref.shape
    tmp[...] = column(qp_ref[...].astype(F32), LANES)
    pos_q = tmp[pl.ds(sc_ref[4], blk, stride=rows // blk), :]
    pos_k = key_positions(sc_ref, off_ref)
    for i in range(0, keys, LANES):
        mask_ref[:, i : i + LANES] = jnp.where(pos_k[:, i : i + LANES] <= pos_q, 0.0, NEG_FILL)
    for head in range(out_ref.shape[0]):
        s = head_scores(q_ref, k_ref, head) + bias[...]
        top = jnp.max(s, axis=0, keepdims=True)
        out_ref[head : head + 1, :] = top + jnp.log(jnp.sum(jnp.exp(s - top), axis=0, keepdims=True))


def scores_lse(sc, queries, attn_keys, off, qp, n_head):
    rows, keys = qp.shape[1], off.shape[1]
    heads = queries.shape[1] // HEAD_DIM
    return pl.pallas_call(
        lse_kernel,
        in_specs=[SMEM_SPEC] + [VMEM_SPEC] * 4,
        out_specs=[VMEM_SPEC] * 2,
        out_shape=[
            jax.ShapeDtypeStruct((heads, rows), F32),
            jax.ShapeDtypeStruct((rows // n_head, keys), F32),
        ],
        scratch_shapes=[pltpu.VMEM((keys, rows), F32), pltpu.VMEM((rows, LANES), F32)],
        compiler_params=WIDE_PARAMS,
        name="scores_lse",
    )(sc, queries, attn_keys, off, qp)


def join_kernel(sc_ref, lse_ref, parts_ref, mask_ref, keep_ref, give_ref, logits_ref):
    half, rows = lse_ref.shape[0] // 2, lse_ref.shape[1]
    logits = jnp.sum(parts_ref[...], axis=0) * INV_SCALE + mask_ref[...]
    blk = logits.shape[0]
    logits_ref[...] = logits
    top = jnp.max(logits, axis=1, keepdims=True)
    value = top + jnp.log(jnp.sum(jnp.exp(logits - top), axis=1, keepdims=True))
    value = jnp.broadcast_to(value, (blk, LANES))
    value = jnp.concatenate([value, jnp.zeros((LANES - blk, LANES), F32)], axis=0).T
    for out_ref, core in ((keep_ref, sc_ref[0]), (give_ref, 1 - sc_ref[0])):
        out_ref[:, :rows] = lse_ref[pl.ds(pl.multiple_of(core * half, half), half), :]
        out_ref[:, rows:] = value[:half]


def join_lse(sc, lse, parts, mask):
    heads, rows = lse.shape
    out = jax.ShapeDtypeStruct((heads // 2, rows + LANES), F32)
    return pl.pallas_call(
        join_kernel,
        in_specs=[SMEM_SPEC] + [VMEM_SPEC] * 3,
        out_specs=[VMEM_SPEC] * 3,
        out_shape=[out, out, jax.ShapeDtypeStruct(mask.shape, F32)],
        compiler_params=PARAMS,
        name="join_lse",
    )(sc, lse, parts, mask)


def pair_kernel(mine_ref, got_ref, out_ref):
    both = merge(jnp.stack([mine_ref[...], got_ref[...]]))
    for c in range(out_ref.shape[0]):
        out_ref[c] = both


def pair_merge(mine, got, n_chip):
    return pl.pallas_call(
        pair_kernel,
        in_specs=[VMEM_SPEC] * 2,
        out_specs=VMEM_SPEC,
        out_shape=jax.ShapeDtypeStruct((n_chip, *mine.shape), F32),
        compiler_params=PARAMS,
        name="pair_merge",
    )(mine, got)


def merge_kernel(parts_ref, out_ref):
    out_ref[...] = merge(parts_ref[...])


def merge_parts(parts):
    return pl.pallas_call(
        merge_kernel,
        in_specs=[VMEM_SPEC],
        out_specs=VMEM_SPEC,
        out_shape=jax.ShapeDtypeStruct(parts.shape[1:], F32),
        compiler_params=PARAMS,
        name="merge_parts",
    )(parts)


def probs_kernel(
    sc_ref, q_ref, k_ref, off_ref, qp_ref, mine_ref, other_ref, b1, b2, b3, out_ref, bias, lse, tr
):
    fill_bias(bias, sc_ref, off_ref, qp_ref)
    half, rows = mine_ref.shape[0], lse.shape[1]
    for ref, core in ((mine_ref, sc_ref[0]), (other_ref, 1 - sc_ref[0])):
        lse[pl.ds(pl.multiple_of(core * half, half), half), :] = ref[:, :rows]
    total = None
    for head in range(0, lse.shape[0], 2):
        pair = [
            jnp.exp(head_scores(q_ref, k_ref, h) + bias[...] - lse[h : h + 1, :]) for h in (head, head + 1)
        ]
        total = pair[0] + pair[1] if total is None else total + (pair[0] + pair[1])
    split_rows(tr, out_ref, total)


def probs_sum(sc, queries, attn_keys, off, qp, mine, other, blocks, n_head):
    rows, keys = qp.shape[1], off.shape[1]
    heads = queries.shape[1] // HEAD_DIM
    return pl.pallas_call(
        probs_kernel,
        in_specs=[SMEM_SPEC] + [VMEM_SPEC] * 6 + [ANY_SPEC] * 3,
        out_specs=VMEM_SPEC,
        out_shape=jax.ShapeDtypeStruct((n_head, rows // n_head, keys), F32),
        scratch_shapes=[
            pltpu.VMEM((keys, rows), F32),
            pltpu.VMEM((heads, rows), F32),
            pltpu.VMEM((rows * keys // LANES, LANES), F32),
        ],
        compiler_params=PARAMS,
        name="probs_sum",
    )(sc, queries, attn_keys, off, qp, mine, other, *blocks)


def step_kernel(sc_ref, target_ref, logits_ref, lse_ref, wide_ref, x1_ref, x2_ref, x3_ref, x0_ref, tmp, turn):
    target = jnp.sum(target_ref[...], axis=0) * (1.0 / HEADS)
    blk, keys = target.shape
    rows = lse_ref.shape[1] - LANES
    lse = lse_ref[:8, rows:].T[:blk, :1]
    step = jnp.exp(logits_ref[...] - lse) - target
    for half in range(keys // LANES):
        part = step[:, half * LANES : (half + 1) * LANES]
        for h in range(wide_ref.shape[0]):
            wide_ref[h, half] = part
        tmp[half] = part
        for z in range(4):
            for x in range(4):
                turn[half, 16 * x + 4 * z : 16 * x + 4 * z + 4, :] = tmp[half, 16 * z + 4 * x : 16 * z + 4 * x + 4, :]
    for k, x_ref in ((1, x1_ref), (2, x2_ref), (3, x3_ref), (0, x0_ref)):
        x_ref[...] = turn[:, pl.ds(pl.multiple_of(lax.rem(sc_ref[1] + k, 4) * 16, 16), 16), :]


def prob_step(sc, target_parts, logits, lse):
    n_head, blk, keys = target_parts.shape
    halves = keys // LANES
    piece = jax.ShapeDtypeStruct((halves, blk // 4, LANES), F32)
    return pl.pallas_call(
        step_kernel,
        in_specs=[SMEM_SPEC] + [VMEM_SPEC] * 3,
        out_specs=[VMEM_SPEC] * 5,
        out_shape=[jax.ShapeDtypeStruct((n_head, halves, blk, LANES), F32)] + [piece] * 4,
        scratch_shapes=[pltpu.VMEM((halves, blk, LANES), F32)] * 2,
        compiler_params=PARAMS,
        name="prob_step",
    )(sc, target_parts, logits, lse)


def around_kernel(p0, p1, p2, p3, first, out_ref):
    for h in range(out_ref.shape[0]):
        for k, ref in enumerate((p0, p1, p2, p3)):
            out_ref[h, k] = ref[...]


def repeat_parts(parts, first, n_head):
    return pl.pallas_call(
        around_kernel,
        in_specs=[VMEM_SPEC] * 4 + [ANY_SPEC],
        out_specs=VMEM_SPEC,
        out_shape=jax.ShapeDtypeStruct((n_head, len(parts), *parts[0].shape), F32),
        compiler_params=PARAMS,
        name="repeat_parts",
    )(*parts, first)


def weight_rows(wt_ref):
    wt = wt_ref[...] * INV_SCALE
    return jnp.concatenate([wt, jnp.zeros((LANES - wt.shape[0], wt.shape[1]), F32)], axis=0).T


def query_kernel(sc_ref, step_ref, iq_ref, wt_ref, i0_ref, i1_ref, i2_ref, i3_ref, first, keep_ref, give_ref, tr, iqs, acc, w_ref):
    w_ref[...] = weight_rows(wt_ref)
    n_head, n_x, quarters, each, _ = step_ref.shape
    size = each * n_head
    block = size // 4
    jl = iq_ref.shape[1] // IDIM
    starts = [pl.multiple_of(4 * block * z + block * sc_ref[1], block) for z in range(4)]
    w = jnp.concatenate([w_ref[pl.ds(b, block), :] for b in starts], axis=0)
    for j in range(jl):
        for z, b in enumerate(starts):
            at = j * size + block * z
            iqs[at : at + block, :] = iq_ref[pl.ds(b, block), j * IDIM : (j + 1) * IDIM]
    total = None
    for k, ik_ref in enumerate((i0_ref, i1_ref, i2_ref, i3_ref)):
        for c in range(quarters):
            for h in range(n_head):
                tr[pl.ds((k * quarters + c) * size + h, each, stride=n_head), :] = step_ref[h, k, c]
        step = jnp.concatenate(
            [tr[(k * quarters + c) * size : (k * quarters + c + 1) * size, :] for c in range(quarters)], axis=1
        )
        ik = ik_ref[...].astype(BF16)
        act = dot_t(iqs[...], ik)
        terms = jnp.concatenate(
            [
                jnp.where(act[j * size : (j + 1) * size] > 0.0, step * w[:, j : j + 1], 0.0).astype(BF16)
                for j in range(jl)
            ],
            axis=0,
        )
        part = jnp.dot(terms, ik, preferred_element_type=F32)
        total = part if total is None else total + part
    acc[...] = total
    piece = block // 2
    for out_ref, core in ((give_ref, 1 - sc_ref[0]), (keep_ref, sc_ref[0])):
        for i, k in enumerate((1, 2, 3, 0)):
            z = lax.rem(sc_ref[2] + k, 4)
            for j in range(jl):
                at = pl.multiple_of(j * size + z * block + core * piece, piece)
                out_ref[i * piece : (i + 1) * piece, j * IDIM : (j + 1) * IDIM] = acc[pl.ds(at, piece), :]


def query_pieces(sc, step, iq, wt, blocks, first):
    n_head, n_x, quarters, each, _ = step.shape
    size = each * n_head
    jl = iq.shape[1] // IDIM
    out = jax.ShapeDtypeStruct((size // 2, iq.shape[1]), F32)
    return pl.pallas_call(
        query_kernel,
        in_specs=[SMEM_SPEC] + [VMEM_SPEC] * 7 + [ANY_SPEC],
        out_specs=[VMEM_SPEC] * 2,
        out_shape=[out] * 2,
        scratch_shapes=[
            pltpu.VMEM((n_x * quarters * size, LANES), F32),
            pltpu.VMEM((size * jl, IDIM), BF16),
            pltpu.VMEM((size * jl, IDIM), F32),
            pltpu.VMEM((iq.shape[0], LANES), F32),
        ],
        compiler_params=PARAMS,
        name="query_pieces",
    )(sc, step, iq, wt, *blocks, first)


def fold_kernel(keep_ref, got_ref, o1_ref, o2_ref, o3_ref, o0_ref):
    piece = o0_ref.shape[0]
    for i, out_ref in enumerate((o1_ref, o2_ref, o3_ref, o0_ref)):
        out_ref[...] = keep_ref[i * piece : (i + 1) * piece] + got_ref[i * piece : (i + 1) * piece]


def fold(keep, got):
    out = jax.ShapeDtypeStruct((keep.shape[0] // 4, keep.shape[1]), F32)
    return pl.pallas_call(
        fold_kernel,
        in_specs=[VMEM_SPEC] * 2,
        out_specs=[VMEM_SPEC] * 4,
        out_shape=[out] * 4,
        compiler_params=PARAMS,
        name="fold",
    )(keep, got)


def key_kernel(step_ref, iq_ref, ik_ref, wt_ref, out_ref, tr):
    n, halves, blk, _ = step_ref.shape
    turned = []
    for c in range(halves):
        base = c * n * blk
        for h in range(n):
            tr[pl.ds(base + h, blk, stride=n), :] = step_ref[h, c]
        turned.append(tr[base : base + n * blk, :].T)
    step = jnp.concatenate(turned, axis=0)
    ik = ik_ref[...].astype(BF16)
    total = None
    for j in range(wt_ref.shape[0]):
        iq = iq_ref[:, j * IDIM : (j + 1) * IDIM]
        act = dot_t(ik, iq)
        terms = jnp.where(act > 0.0, step * (wt_ref[j : j + 1, :] * INV_SCALE), 0.0).astype(BF16)
        part = jnp.dot(terms, iq, preferred_element_type=F32)
        total = part if total is None else total + part
    out_ref[...] = total


def key_part_grad(step, iq, ik, wt):
    n, halves, blk, _ = step.shape
    return pl.pallas_call(
        key_kernel,
        in_specs=[VMEM_SPEC] * 4,
        out_specs=VMEM_SPEC,
        out_shape=jax.ShapeDtypeStruct(ik.shape, F32),
        scratch_shapes=[pltpu.VMEM((n * halves * blk, LANES), F32)],
        compiler_params=PARAMS,
        name="key_part_grad",
    )(step, iq, ik, wt)


def shards(queries, attn_keys, index_queries, index_keys, head_weights, query_pos, key_offset):
    n_head, n_chip = lax.axis_size(HEAD), lax.axis_size(CHIP)
    sc = jnp.stack([lax.axis_index(a) for a in ("core", "x", "z_hi", CTX, HEAD)]).astype(jnp.int32)

    off, qp = key_offset[None, :], query_pos[None, :]
    w_t = head_weights.T

    index, ik = front(index_queries, index_keys, w_t, n_head)
    index = lax.all_to_all(index, HEAD, 0, 0)

    lse, mask = scores_lse(sc, queries, attn_keys, off, qp, n_head)
    mine, give, logits = join_lse(sc, lse, index, mask)
    mine = pair_merge(mine, shift(give, "core", 2, 1), n_chip)
    mine = merge_parts(lax.all_to_all(mine, CHIP, 0, 0))
    other = shift(mine, "core", 2, 1)
    around = [shift(ik, "x", 4, k) for k in range(1, 4)]
    target = probs_sum(sc, queries, attn_keys, off, qp, mine, other, around, n_head)
    target = lax.all_to_all(target, HEAD, 0, 0)

    step_key, *pieces = prob_step(sc, target, logits, mine)
    step_key = lax.all_to_all(step_key, HEAD, 0, 0)
    pieces = [pieces[3]] + [shift(pieces[k - 1], "x", 4, k) for k in range(1, 4)]
    step_query = lax.all_to_all(repeat_parts(pieces, step_key, n_head), HEAD, 0, 0)

    key_part = key_part_grad(step_key, index_queries, ik, w_t)
    key_part = key_part + shift(key_part, "z_lo", 2, 1)
    key_grad = key_part
    for k in range(1, 4):
        key_grad = key_grad + shift(key_part, "y", 4, k)

    keep, give = query_pieces(sc, step_query, index_queries, w_t, [ik] + around, key_part)
    p1, p2, p3, query_grad = fold(keep, shift(give, "core", 2, 1))
    query_grad = query_grad + shift(p1, "z_hi", 4, 1) + shift(p2, "z_hi", 4, 2) + shift(p3, "z_hi", 4, 3)
    return (query_grad, key_grad)


def solution(mesh):
    mesh = Mesh(mesh.devices.reshape(2, 4, 4, 4, 2), AXES)
    in_specs = (
        P(None, HEAD),
        P(CTX, HEAD),
        P(None, HEAD),
        P(CTX, None),
        P(None, HEAD),
        P(),
        P(CTX),
    )
    out_specs = (P(CTX, HEAD), P(CTX, None))
    return jax.shard_map(shards, mesh=mesh, in_specs=in_specs, out_specs=out_specs, check_vma=False)
```
